256 devices in a mesh: head: 16 (over z, core), seq: 16 (over x, y).
Axes of the slice: x: 4, y: 4, z: 8, core: 2. Of those that a mesh axis runs over, the one named last changes fastest.
Arguments:
- queries: bfloat16 [8192, 2048], P(('seq', 'head')), may hold values from -6 to 6
- key_vectors: bfloat16 [8192, 2048], P(('seq', 'head')), may hold values from -6 to 6
- value_vectors: bfloat16 [8192, 2048], P(('seq', 'head')), may hold values from -6 to 6
- out_grad: bfloat16 [8192, 2048], P(('seq', 'head')), may hold values from -6 to 6
- key_tiles: int32 [16, 64, 38], replicated, may hold values from 0 to 63, as said below
- tile_count: int32 [16, 64], replicated, may hold values from 4 to 38, as said below
Outputs:
- attended: bfloat16 [8192, 2048], P(('seq', 'head'))
- grad_queries: bfloat16 [8192, 2048], P(('seq', 'head'))
- grad_keys: bfloat16 [8192, 2048], P(('seq', 'head'))
- grad_values: bfloat16 [8192, 2048], P(('seq', 'head'))
The draws below stay inside these ranges and needn't reach their ends.
Inputs may be any that keep to these rules, and one draw needn't show every extreme that they name: key_tiles[h, i, 0] is i; the 38 entries of one list are distinct; only the first tile_count[h, i] entries are active. `tile_count`: each list covers 5 to 60 percent of the clip's tiles; the value 38 is taken in every draw.
All inputs are finite; a program needn't handle non-finite values.
Results may differ from the reference program's by a relative error of at most 0.029.
Values may be sent and summed in bfloat16 or wider, within the bound.
No kernel may reach another device: no remote copies, remote signals or barrier semaphores. Data moves between devices by JAX's collectives and lax.ppermute only.
A program may use at most 128 MiB of HBM per device.

```python
import math
import jax
import jax.numpy as jnp
from jax import lax

H = 16
DH = 128
TILE = 128
S = 8192
NB = 64
KCAP = 38


def draw_queries(key, part):
    key = jax.random.fold_in(key, 7)
    return jnp.clip(jax.random.normal(key, (S, H * DH), jnp.float32), -6.0, 6.0).astype(jnp.bfloat16)


def draw_key_vectors(key, part):
    key = jax.random.fold_in(key, 9)
    return jnp.clip(jax.random.normal(key, (S, H * DH), jnp.float32), -6.0, 6.0).astype(jnp.bfloat16)


def tile_plan(key):
    order_key, halving_key, factor_key, head_key, block_key = jax.random.split(key, 5)
    block_total = S // TILE
    least_count = (block_total + 19) // 20
    shuffle = jax.random.randint(order_key, (H, block_total, block_total), 0, 1 << 20) * block_total + jnp.arange(block_total, dtype=jnp.int32)[None, None, :]
    diagonal = (jnp.arange(block_total)[:, None] == jnp.arange(block_total)[None, :])[None, :, :]
    ranking = jnp.argsort(jnp.where(diagonal, -1, shuffle), axis=-1).astype(jnp.int32)
    halving = jax.random.randint(halving_key, (H,), 0, 4)
    head_base = jnp.maximum(KCAP // jnp.power(2, halving), 1)
    factor = jax.random.randint(factor_key, (H, block_total), 2, 7)
    counts = jnp.clip(head_base[:, None] * factor // 4, least_count, KCAP)
    peak_head = jax.random.randint(head_key, (), 0, H)
    peak_block = jax.random.randint(block_key, (), 0, block_total)
    peak_spot = (jnp.arange(H)[:, None] == peak_head) & (jnp.arange(block_total)[None, :] == peak_block)
    counts = jnp.where(peak_spot, KCAP, counts).astype(jnp.int32)
    return (ranking[:, :, :KCAP], counts)


def draw_key_tiles(key, part):
    listing, counts = tile_plan(key)
    return listing


def draw_tile_count(key, part):
    listing, counts = tile_plan(key)
    return counts


def steps_of(stream_key, dims, shards, smallest, top_value):
    gain, own = 1.0, jax.random.fold_in(stream_key, 6)
    for axis_at, parts in shards:
        heights = jnp.exp(jax.random.uniform(jax.random.fold_in(own, axis_at), (parts,), jnp.float32, smallest / len(shards), top_value / len(shards)))
        gain = gain * jnp.repeat(heights, dims[axis_at] // parts).reshape([-1 if axis == axis_at else 1 for axis in range(len(dims))])
    return gain


def gaussian(rng, dims, width, bound, cuts=(), kind=jnp.bfloat16):
    result = width * jax.random.normal(rng, dims, jnp.float32)
    if cuts:
        result = result * steps_of(rng, dims, cuts, -0.22, 0.18)
    return jnp.clip(result, -bound, bound).astype(kind)


def setup_inputs(seed: int = 0) -> dict:
    seeds = jax.random.split(jax.random.key(seed), 7)
    return {
        "queries": draw_queries(jax.random.fold_in(seeds[6], 71), 0),
        "key_vectors": draw_key_vectors(jax.random.fold_in(seeds[6], 71), 0),
        "value_vectors": gaussian(seeds[2], (S, H * DH), 1.0, 6.0, ((0, 256),)),
        "out_grad": gaussian(seeds[3], (S, H * DH), 1.0, 6.0, ((0, 256),)),
        "key_tiles": draw_key_tiles(jax.random.fold_in(seeds[6], 71), 0),
        "tile_count": draw_tile_count(jax.random.fold_in(seeds[6], 71), 0),
    }


masked_score = -1e+30

def tile_graph(key_tiles, tile_count):
    head_total, block_total, slot_total = key_tiles.shape
    live = (jnp.arange(slot_total, dtype=jnp.int32)[None, None, :] < tile_count[:, :, None]).astype(jnp.int32)
    head_ids = jnp.broadcast_to(jnp.arange(head_total, dtype=jnp.int32)[:, None, None], key_tiles.shape)
    row_ids = jnp.broadcast_to(jnp.arange(block_total, dtype=jnp.int32)[None, :, None], key_tiles.shape)
    empty = jnp.zeros((head_total, block_total, block_total), jnp.int32)
    return empty.at[head_ids, row_ids, key_tiles].max(live)

def one_head(operands):
    query_head, key_head, value_head, grad_head, graph_head = operands
    inv_root = 1.0 / math.sqrt(DH)

    def per_block(running, block_at):
        key_grad, value_grad = running
        row_start = (block_at * TILE).astype(jnp.int32)
        query_rows = lax.dynamic_slice_in_dim(query_head, row_start, TILE, 0)
        grad_rows = lax.dynamic_slice_in_dim(grad_head, row_start, TILE, 0)
        allowed = (jnp.repeat(graph_head[block_at], TILE) > 0)[None, :]
        scores = jnp.dot(query_rows, key_head.T, preferred_element_type=jnp.float32) * inv_root
        masked = jnp.where(allowed, scores, masked_score)
        row_top = lax.optimization_barrier(jnp.max(masked, axis=1, keepdims=True))
        row_lse = row_top + jnp.log(lax.optimization_barrier(jnp.sum(jnp.exp(masked - row_top), axis=1, keepdims=True)))
        weights = jnp.exp(jnp.where(allowed, scores - row_lse, masked_score))
        weights_low = weights.astype(jnp.bfloat16)
        out_rows = jnp.dot(weights_low, value_head, preferred_element_type=jnp.float32).astype(jnp.bfloat16)
        row_delta = lax.optimization_barrier(jnp.sum(grad_rows.astype(jnp.float32) * out_rows.astype(jnp.float32), axis=1, keepdims=True))
        dprobs = jnp.dot(grad_rows, value_head.T, preferred_element_type=jnp.float32)
        dscores = (weights * (dprobs - row_delta) * inv_root).astype(jnp.bfloat16)
        query_out = jnp.dot(dscores, key_head, preferred_element_type=jnp.float32).astype(jnp.bfloat16)
        key_grad = key_grad + jnp.dot(dscores.T, query_rows, preferred_element_type=jnp.float32)
        value_grad = value_grad + jnp.dot(weights_low.T, grad_rows, preferred_element_type=jnp.float32)
        return ((key_grad, value_grad), (out_rows, query_out))
    zero_grad = jnp.zeros((S, DH), jnp.float32)
    finals, stacked = lax.scan(per_block, (zero_grad, zero_grad), jnp.arange(NB, dtype=jnp.int32))
    attended_rows = stacked[0].reshape(S, DH)
    query_rows_grad = stacked[1].reshape(S, DH)
    return (attended_rows, query_rows_grad, finals[0].astype(jnp.bfloat16), finals[1].astype(jnp.bfloat16))

def split_heads(matrix):
    return matrix.reshape(S, H, DH).transpose(1, 0, 2)

def join_heads(stacked):
    return stacked.transpose(1, 0, 2).reshape(S, H * DH)

def reference(queries, key_vectors, value_vectors, out_grad, key_tiles, tile_count):
    tile_mask = tile_graph(key_tiles, tile_count)
    results = lax.map(one_head, (split_heads(queries), split_heads(key_vectors), split_heads(value_vectors), split_heads(out_grad), tile_mask))
    return (join_heads(results[0]), join_heads(results[1]), join_heads(results[2]), join_heads(results[3]))
```

```python
import math

import jax
import jax.numpy as jnp
from jax import lax
from jax.experimental import pallas as pl
from jax.experimental.pallas import tpu as pltpu
from jax.sharding import PartitionSpec as P

DH = 128
TILE = 128
SCALE = 1.0 / math.sqrt(DH)
LOG2E = math.log2(math.e)
C1 = SCALE * LOG2E
QB = 256
KC = 512
NEG = -1e30
SHIFTS = (1, 3, 2)
BACK = (0, 1, 3, 2)

NT = (((1,), (1,)), ((), ()))
NN = (((1,), (0,)), ((), ()))


def dot(a, b, dims):
    return lax.dot_general(a, b, dims, preferred_element_type=jnp.float32)


def stats_kernel(*refs):
    qg, kv = refs[0:4], refs[4:8]
    bias_ref = refs[8]
    stat_ref, out_ref = refs[9:11]
    q_s, g_s, k_s, vt_s, xa_s, xb_s = refs[11:17]
    for j in range(4):
        rows = slice(j * 512, (j + 1) * 512)
        q_s[rows] = qg[j][:, 0].reshape(512, DH)
        g_s[rows] = qg[j][:, 1].reshape(512, DH)
        k_s[rows] = kv[j][:, 0].reshape(512, DH)
        vt_s[:, rows] = kv[j][:, 1].reshape(512, DH).T

    def score(qb, x_s):
        start = pl.multiple_of(qb * QB, QB)
        q = q_s[pl.ds(start, QB)]
        top = jnp.full((1, QB), NEG, jnp.float32)
        for c in range(4):
            s = dot(k_s[c * KC:(c + 1) * KC], q, NT) * C1
            bias = bias_ref[c * 4:(c + 1) * 4, pl.ds(start, QB)]
            x = (s.reshape(4, TILE, QB) + bias[:, None, :]).reshape(KC, QB)
            x_s[c * KC:(c + 1) * KC] = x
            top = jnp.maximum(top, jnp.max(x, axis=0, keepdims=True))
        return top

    def finish(qb, x_s, top):
        start = pl.multiple_of(qb * QB, QB)
        mass = jnp.zeros((1, QB), jnp.float32)
        acc = jnp.zeros((DH, QB), jnp.float32)
        for c in range(4):
            e = jnp.exp2(x_s[c * KC:(c + 1) * KC] - top)
            mass = mass + jnp.sum(e, axis=0, keepdims=True)
            acc = acc + dot(vt_s[:, c * KC:(c + 1) * KC], e.astype(jnp.bfloat16), NN)
        gt = g_s[pl.ds(start, QB)].astype(jnp.float32).T
        delta = jnp.sum(gt * acc, axis=0, keepdims=True)
        stat_ref[0, pl.ds(qb, 1)] = top
        stat_ref[1, pl.ds(qb, 1)] = mass
        stat_ref[2, pl.ds(qb, 1)] = delta
        out_ref[:, pl.ds(start, QB)] = acc

    def pair(i, top):
        top_b = score(2 * i + 1, xb_s)
        finish(2 * i, xa_s, top)
        top_a = score(jnp.minimum(2 * i + 2, 7), xa_s)
        finish(2 * i + 1, xb_s, top_b)
        return top_a

    lax.fori_loop(0, 4, pair, score(0, xa_s))


def grad_kernel(*refs):
    qg, kv = refs[0:4], refs[4:8]
    bias_ref, acc_ref = refs[8:10]
    stats = refs[10:14]
    o_ref, dq_ref, dk_ref, dv_ref = refs[14:18]
    q_s, g_s, k_s, v_s, kt_s, dk_s, dv_s, lse_s, delta_s, fade_s = refs[18:28]
    for j in range(4):
        rows = slice(j * 512, (j + 1) * 512)
        q_s[rows] = qg[j][:, 0].reshape(512, DH)
        g_s[rows] = qg[j][:, 1].reshape(512, DH)
        k = kv[j][:, 0].reshape(512, DH)
        k_s[rows] = k
        kt_s[:, rows] = k.T
        v_s[rows] = kv[j][:, 1].reshape(512, DH)
    tops, masses, deltas = [], [], []
    for shift, stat in zip((0,) + SHIFTS, stats):
        order = [BACK.index((BACK[j] - shift) % 4) for j in range(4)]
        for held, n in ((tops, 0), (masses, 1), (deltas, 2)):
            held.append(jnp.concatenate([stat[n, 2 * p:2 * p + 2] for p in order], axis=0))
    top = jnp.maximum(jnp.maximum(tops[0], tops[1]), jnp.maximum(tops[2], tops[3]))
    fades = [jnp.exp2(t - top) for t in tops]
    mass = sum(m * f for m, f in zip(masses, fades))
    inv_mass = 1.0 / mass
    delta_s[...] = sum(d * f for d, f in zip(deltas, fades)) * inv_mass
    lse_s[...] = top + jnp.log2(mass)
    fade_s[...] = fades[0] * inv_mass
    dk_s[...] = jnp.zeros_like(dk_s)
    dv_s[...] = jnp.zeros_like(dv_s)

    def block(qb, carry):
        start = pl.multiple_of(qb * QB, QB)
        q = q_s[pl.ds(start, QB)]
        g = g_s[pl.ds(start, QB)]
        lse = lse_s[pl.ds(qb, 1)]
        delta = delta_s[pl.ds(qb, 1)]
        out = acc_ref[:, pl.ds(start, QB)] * fade_s[pl.ds(qb, 1)]
        o_ref[pl.ds(start, QB)] = out.T.astype(jnp.bfloat16)
        dqt = jnp.zeros((DH, QB), jnp.float32)
        for c in range(4):
            rows = slice(c * KC, (c + 1) * KC)
            s = dot(k_s[rows], q, NT) * C1
            shift = bias_ref[c * 4:(c + 1) * 4, pl.ds(start, QB)] - lse
            w = jnp.exp2((s.reshape(4, TILE, QB) + shift[:, None, :]).reshape(KC, QB))
            dp = dot(v_s[rows], g, NT)
            ds = (w * (dp - delta)).astype(jnp.bfloat16)
            dv_s[rows] += dot(w.astype(jnp.bfloat16), g, NN)
            dk_s[rows] += dot(ds, q, NN)
            dqt = dqt + dot(kt_s[:, rows], ds, NN)
        dq_ref[pl.ds(start, QB)] = (dqt * SCALE).T.astype(jnp.bfloat16)
        return carry

    lax.fori_loop(0, 8, block, 0)
    dk_ref[...] = (dk_s[...] * SCALE).astype(jnp.bfloat16)
    dv_ref[...] = dv_s[...].astype(jnp.bfloat16)


VM = pl.BlockSpec(memory_space=pltpu.VMEM)
PARAMS = pltpu.CompilerParams(vmem_limit_bytes=40 * 1024 * 1024)


def run_stats(qg, kv, bias):
    return pl.pallas_call(
        stats_kernel,
        out_shape=(
            jax.ShapeDtypeStruct((3, 8, QB), jnp.float32),
            jax.ShapeDtypeStruct((DH, 2048), jnp.float32),
        ),
        in_specs=[VM] * 9,
        out_specs=(VM, VM),
        scratch_shapes=[pltpu.VMEM((2048, DH), jnp.bfloat16)] * 3
        + [pltpu.VMEM((DH, 2048), jnp.bfloat16)]
        + [pltpu.VMEM((2048, QB), jnp.float32)] * 2,
        compiler_params=PARAMS,
        name="stats",
    )(*qg, *kv, bias)


def run_grads(qg, kv, bias, acc, stats):
    half = jax.ShapeDtypeStruct((2048, DH), jnp.bfloat16)
    return pl.pallas_call(
        grad_kernel,
        out_shape=(half,) * 4,
        in_specs=[VM] * 14,
        out_specs=(VM,) * 4,
        scratch_shapes=[pltpu.VMEM((2048, DH), jnp.bfloat16)] * 4
        + [pltpu.VMEM((DH, 2048), jnp.bfloat16)]
        + [pltpu.VMEM((2048, DH), jnp.float32)] * 2
        + [pltpu.VMEM((8, QB), jnp.float32)] * 3,
        compiler_params=PARAMS,
        name="grads",
    )(*qg, *kv, bias, acc, *stats)


def ring(n, k):
    return [(i, (i + k) % n) for i in range(n)]


def per_device(queries, key_vectors, value_vectors, out_grad, key_tiles, tile_count):
    x_at = lax.axis_index("x")
    y_at = lax.axis_index("y")
    head_at = lax.axis_index("z") * 2 + lax.axis_index("core")

    back = jnp.array(BACK, jnp.int32)
    q_tiles = x_at * 16 + ((y_at - back) % 4)[:, None] * 4 + jnp.arange(4, dtype=jnp.int32)[None]
    k_tiles = ((x_at - back) % 4)[:, None] * 16 + y_at * 4 + jnp.arange(4, dtype=jnp.int32)[None]
    lists = lax.dynamic_slice(key_tiles, (head_at, 0, 0), (1, 64, key_tiles.shape[2]))[0]
    counts = lax.dynamic_slice(tile_count, (head_at, 0), (1, 64))[0]
    live = jnp.arange(key_tiles.shape[2], dtype=jnp.int32)[None, :] < counts[:, None]
    lists = jnp.where(live, lists, -1)[q_tiles.reshape(16)]
    hit = jnp.any(lists[None, :, :] == k_tiles.reshape(16)[:, None, None], axis=2)
    bias = jnp.repeat(jnp.where(hit, 0.0, NEG).astype(jnp.float32), TILE, axis=1)

    def by_head(a):
        return a.reshape(32, 16, DH).transpose(1, 0, 2)

    packed = jnp.stack(
        [by_head(queries), by_head(out_grad), by_head(key_vectors), by_head(value_vectors)], axis=1
    )
    got = lax.all_to_all(packed, ("z", "core"), split_axis=0, concat_axis=0, tiled=True)
    qg_own, kv_own = got[:, 0:2], got[:, 2:4]
    qg = [qg_own] + [lax.ppermute(qg_own, "y", ring(4, k)) for k in SHIFTS]
    kv = [kv_own] + [lax.ppermute(kv_own, "x", ring(4, k)) for k in SHIFTS]
    stat, acc = run_stats(qg, kv, bias)
    stats = [stat] + [lax.ppermute(stat, "y", ring(4, k)) for k in SHIFTS]
    out, dq, dk, dv = run_grads(qg, kv, bias, acc, stats)

    def scatter_pair(a, b, axis):
        pa, pb = a.reshape(4, 512, DH), b.reshape(4, 512, DH)
        both = [jnp.stack([pa[j], pb[j]]) for j in range(4)]
        total = both[0].astype(jnp.float32)
        for j, k in enumerate((3, 1, 2)):
            total = total + lax.ppermute(both[j + 1], axis, ring(4, k)).astype(jnp.float32)
        return total.astype(jnp.bfloat16).reshape(2, 16, 32, DH)

    od = scatter_pair(out, dq, "y")
    kvd = scatter_pair(dk, dv, "x")
    send = jnp.concatenate([od, kvd], axis=0).transpose(1, 0, 2, 3)
    back_home = lax.all_to_all(send, ("z", "core"), split_axis=0, concat_axis=0, tiled=True)

    def by_row(a):
        return a.transpose(1, 0, 2).reshape(32, 16 * DH)

    return tuple(by_row(back_home[:, j]) for j in range(4))


def solution(mesh):
    grid = jax.sharding.Mesh(mesh.devices.reshape(8, 2, 4, 4), ("z", "core", "x", "y"))
    rows = P(("x", "y", "z", "core"), None)
    return jax.shard_map(
        per_device,
        mesh=grid,
        in_specs=(rows, rows, rows, rows, P(), P()),
        out_specs=(rows,) * 4,
        check_vma=False,
    )
```

```python
import math

import jax
import jax.numpy as jnp
from jax import lax
from jax.experimental import pallas as pl
from jax.experimental.pallas import tpu as pltpu
from jax.sharding import PartitionSpec as P
from jax.sharding import PartitionSpec as P

DH = 128
TILE = 128
SCALE = 1.0 / math.sqrt(DH)
LOG2E = math.log2(math.e)
C1 = SCALE * LOG2E
QB = 256
KC = 512
NEG = -1e30
SHIFTS = (1, 3, 2)
BACK = (0, 1, 3, 2)
HALF = TILE // 2

NT = (((1,), (1,)), ((), ()))
NN = (((1,), (0,)), ((), ()))


def dot(a, b, dims):
    return lax.dot_general(a, b, dims, preferred_element_type=jnp.float32)


def load_queries(place, qg, q5_s, g5_s):
    for j in range(4):
        y1_at, core_at = place[0] ^ (j // 2), place[1] ^ (j % 2)
        q5_s[y1_at, :, core_at] = qg[j][:, 0]
        g5_s[y1_at, :, core_at] = qg[j][:, 1]
    return q5_s.reshape(2048, DH), g5_s.reshape(2048, DH)


def stats_kernel(*refs):
    place, qg, kv = refs[0], refs[1:5], refs[5:9]
    bias_ref = refs[9]
    stat_ref, out_ref, e_ref = refs[10:13]
    q5_s, g5_s, k_s, vt_s, xa_s, xb_s = refs[13:19]
    q_s, g_s = load_queries(place, qg, q5_s, g5_s)
    for j in range(4):
        rows = slice(j * 512, (j + 1) * 512)
        k_s[rows] = kv[j][:, 0].reshape(512, DH)
        vt_s[:, rows] = kv[j][:, 1].reshape(512, DH).T

    def score(qb, x_s):
        start = pl.multiple_of(qb * QB, QB)
        q = q_s[pl.ds(start, QB)]
        top = jnp.full((1, QB), NEG, jnp.float32)
        for c in range(4):
            s = dot(k_s[c * KC:(c + 1) * KC], q, NT) * C1
            bias = bias_ref[c * 8:(c + 1) * 8, pl.ds(start, QB)]
            x = (s.reshape(8, HALF, QB) + bias[:, None, :]).reshape(KC, QB)
            x_s[c * KC:(c + 1) * KC] = x
            top = jnp.maximum(top, jnp.max(x, axis=0, keepdims=True))
        return top

    def finish(qb, x_s, top):
        start = pl.multiple_of(qb * QB, QB)
        mass = jnp.zeros((1, QB), jnp.float32)
        acc = jnp.zeros((DH, QB), jnp.float32)
        for c in range(4):
            rows = slice(c * KC, (c + 1) * KC)
            e = jnp.exp2(x_s[rows] - top)
            mass = mass + jnp.sum(e, axis=0, keepdims=True)
            low = e.astype(jnp.bfloat16)
            e_ref[rows, pl.ds(start, QB)] = low
            acc = acc + dot(vt_s[:, rows], low, NN)
        gt = g_s[pl.ds(start, QB)].astype(jnp.float32).T
        delta = jnp.sum(gt * acc, axis=0, keepdims=True)
        stat_ref[0, pl.ds(qb, 1)] = top
        stat_ref[1, pl.ds(qb, 1)] = mass
        stat_ref[2, pl.ds(qb, 1)] = delta
        out_ref[:, pl.ds(start, QB)] = acc

    def pair(i, top):
        top_b = score(2 * i + 1, xb_s)
        finish(2 * i, xa_s, top)
        top_a = score(jnp.minimum(2 * i + 2, 7), xa_s)
        finish(2 * i + 1, xb_s, top_b)
        return top_a

    lax.fori_loop(0, 4, pair, score(0, xa_s), unroll=2)


def grad_kernel(*refs):
    place, qg, kv = refs[0], refs[1:5], refs[5:9]
    e_ref, acc_ref = refs[9:11]
    stats = refs[11:15]
    keep_ref, send_ref, dk_ref, dv_ref = refs[15:19]
    q5_s, g5_s, o5_s, dq5_s, v_s, kt_s, dk_s, dv_s, delta_s, fade_s = refs[19:29]
    q_s, g_s = load_queries(place, qg, q5_s, g5_s)
    o_s, dq_s = o5_s.reshape(2048, DH), dq5_s.reshape(2048, DH)
    for j in range(4):
        rows = slice(j * 512, (j + 1) * 512)
        kt_s[:, rows] = kv[j][:, 0].reshape(512, DH).T
        v_s[rows] = kv[j][:, 1].reshape(512, DH)
    tops, masses, deltas = [[s[n] for s in stats] for n in range(3)]
    top = jnp.maximum(jnp.maximum(tops[0], tops[1]), jnp.maximum(tops[2], tops[3]))
    fades = [jnp.exp2(t - top) for t in tops]
    mass = sum(m * f for m, f in zip(masses, fades))
    inv_mass = 1.0 / mass
    delta_s[...] = sum(d * f for d, f in zip(deltas, fades)) * inv_mass
    fade_s[...] = fades[0] * inv_mass
    dk_s[...] = jnp.zeros_like(dk_s)
    dv_s[...] = jnp.zeros_like(dv_s)

    def block(qb, carry):
        start = pl.multiple_of(qb * QB, QB)
        q = q_s[pl.ds(start, QB)]
        g = g_s[pl.ds(start, QB)]
        delta = delta_s[pl.ds(qb, 1)]
        fade = fade_s[pl.ds(qb, 1)]
        gf = (g.astype(jnp.float32).T * fade).T.astype(jnp.bfloat16)
        out = acc_ref[:, pl.ds(start, QB)] * fade
        o_s[pl.ds(start, QB)] = out.T.astype(jnp.bfloat16)
        dqt = jnp.zeros((DH, QB), jnp.float32)
        for c in range(4):
            rows = slice(c * KC, (c + 1) * KC)
            e = e_ref[rows, pl.ds(start, QB)]
            dp = dot(v_s[rows], g, NT)
            ds = (e.astype(jnp.float32) * ((dp - delta) * fade)).astype(jnp.bfloat16)
            dv_s[rows] += dot(e, gf, NN)
            dk_s[rows] += dot(ds, q, NN)
            dqt = dqt + dot(kt_s[:, rows], ds, NN)
        dq_s[pl.ds(start, QB)] = (dqt * SCALE).T.astype(jnp.bfloat16)
        return carry

    lax.fori_loop(0, 8, block, 0, unroll=8)
    for n, rows5 in enumerate((o5_s, dq5_s)):
        for far in range(2):
            keep_ref[n, far] = rows5[place[0] ^ far, :, place[1]]
            send_ref[n, far] = rows5[place[0] ^ far, :, 1 - place[1]]
    dk_ref[...] = (dk_s[...] * SCALE).astype(jnp.bfloat16)
    dv_ref[...] = dv_s[...].astype(jnp.bfloat16)


VM = pl.BlockSpec(memory_space=pltpu.VMEM)
SM = pl.BlockSpec(memory_space=pltpu.SMEM)
PARAMS = pltpu.CompilerParams(vmem_limit_bytes=16 * 1024 * 1024)
ROWS5 = pltpu.VMEM((2, 16, 2, 32, DH), jnp.bfloat16)


def run_stats(place, qg, kv, bias):
    return pl.pallas_call(
        stats_kernel,
        out_shape=(
            jax.ShapeDtypeStruct((3, 8, QB), jnp.float32),
            jax.ShapeDtypeStruct((DH, 2048), jnp.float32),
            jax.ShapeDtypeStruct((2048, 2048), jnp.bfloat16),
        ),
        in_specs=[SM] + [VM] * 9,
        out_specs=(VM,) * 3,
        scratch_shapes=[ROWS5] * 2
        + [pltpu.VMEM((2048, DH), jnp.bfloat16), pltpu.VMEM((DH, 2048), jnp.bfloat16)]
        + [pltpu.VMEM((2048, QB), jnp.float32)] * 2,
        compiler_params=PARAMS,
        name="stats",
    )(place, *qg, *kv, bias)


def run_grads(place, qg, kv, e, acc, stats):
    side = jax.ShapeDtypeStruct((2, 2, 16, 32, DH), jnp.bfloat16)
    keys = jax.ShapeDtypeStruct((2048, DH), jnp.bfloat16)
    return pl.pallas_call(
        grad_kernel,
        out_shape=(side, side, keys, keys),
        in_specs=[SM] + [VM] * 14,
        out_specs=(VM,) * 4,
        scratch_shapes=[ROWS5] * 4
        + [pltpu.VMEM((2048, DH), jnp.bfloat16), pltpu.VMEM((DH, 2048), jnp.bfloat16)]
        + [pltpu.VMEM((2048, DH), jnp.float32)] * 2
        + [pltpu.VMEM((8, QB), jnp.float32)] * 2,
        compiler_params=PARAMS,
        name="grads",
    )(place, *qg, *kv, e, acc, *stats)


def ring(n, k):
    return [(i, (i + k) % n) for i in range(n)]


SWAP = [(0, 1), (1, 0)]
HEADS = ("y0", "z")


def per_device(queries, key_vectors, value_vectors, out_grad, key_tiles, tile_count):
    x_at, y1_at, core_at = [lax.axis_index(a) for a in ("x", "y1", "core")]
    head_at = lax.axis_index("y0") * 8 + lax.axis_index("z")
    place = jnp.stack([y1_at, core_at]).astype(jnp.int32)

    back = jnp.array(BACK, jnp.int32)
    tiles = jnp.arange(16, dtype=jnp.int32)
    k_tiles = (((x_at - back) % 4)[:, None] * 16 + y1_at * 8 + tiles[None, :8]).reshape(32)
    slots = key_tiles.shape[2]
    lists = lax.dynamic_slice(key_tiles, (head_at, x_at * 16, 0), (1, 16, slots))[0]
    counts = lax.dynamic_slice(tile_count, (head_at, x_at * 16), (1, 16))[0]
    live = jnp.arange(slots, dtype=jnp.int32)[None, :] < counts[:, None]
    lists = jnp.where(live, lists, -1)
    hit = jnp.any(lists[None, :, :] == k_tiles[:, None, None], axis=2)
    bias = jnp.repeat(jnp.where(hit, 0.0, NEG).astype(jnp.float32), TILE, axis=1)

    def by_head(a):
        return a.reshape(32, 16, DH).transpose(1, 0, 2)

    packed = jnp.stack(
        [by_head(queries), by_head(out_grad), by_head(key_vectors), by_head(value_vectors)], axis=1
    )
    got = lax.all_to_all(packed, HEADS, split_axis=0, concat_axis=0, tiled=True)
    got, bias = lax.optimization_barrier((got, bias))
    qg_own, kv_own = got[:, 0:2], got[:, 2:4]
    kv = [kv_own] + [lax.ppermute(kv_own, "x", ring(4, k)) for k in SHIFTS]
    qg_far = lax.ppermute(qg_own, "y1", SWAP)
    qg = [
        qg_own,
        lax.ppermute(qg_own, "core", SWAP),
        qg_far,
        lax.ppermute(qg_far, "core", SWAP),
    ]
    stat, acc, e = run_stats(place, qg, kv, bias)
    stats = [
        stat,
        lax.ppermute(stat, "core", SWAP),
        lax.ppermute(stat, "y1", SWAP),
        lax.ppermute(stat, ("core", "y1"), [(i, 3 - i) for i in range(4)]),
    ]
    keep, away, dk, dv = run_grads(place, qg, kv, e, acc, stats)

    def pair(a, b, j):
        rows = slice(512 * j, 512 * (j + 1))
        return jnp.stack([a[rows], b[rows]])

    came = [lax.ppermute(pair(dk, dv, j), "x", ring(4, -k)) for j, k in enumerate(BACK) if j]
    near, far = add_core(keep, lax.ppermute(away, "core", SWAP))
    send = add_up(dk, dv, came, near, lax.ppermute(far, "y1", SWAP))
    back_home = lax.all_to_all(send, HEADS, split_axis=0, concat_axis=0, tiled=True)
    return unpack(back_home)


def add_core_kernel(keep_ref, came_ref, near_ref, far_ref):
    for n in range(2):
        for far, out in enumerate((near_ref, far_ref)):
            total = keep_ref[n, far].astype(jnp.float32) + came_ref[n, far].astype(jnp.float32)
            out[n] = total.astype(out.dtype)


def add_core(keep, came):
    return pl.pallas_call(
        add_core_kernel,
        out_shape=(
            jax.ShapeDtypeStruct((2, 16, 32, DH), jnp.float32),
            jax.ShapeDtypeStruct((2, 16, 32, DH), jnp.bfloat16),
        ),
        in_specs=[VM] * 2,
        out_specs=(VM,) * 2,
        compiler_params=PARAMS,
        name="add_core",
    )(keep, came)


def add_kernel(dk_ref, dv_ref, *refs):
    came, near_ref, far_ref, send_ref = refs[0:3], refs[3], refs[4], refs[5]
    for n in range(2):
        rows = near_ref[n] + far_ref[n].astype(jnp.float32)
        send_ref[:, n] = rows.astype(jnp.bfloat16)
    for n, own in enumerate((dk_ref, dv_ref)):
        total = own[0:512].astype(jnp.float32)
        for part in came:
            total = total + part[n].astype(jnp.float32)
        send_ref[:, 2 + n] = total.astype(jnp.bfloat16).reshape(16, 32, DH)


def add_up(dk, dv, came, near, far):
    return pl.pallas_call(
        add_kernel,
        out_shape=jax.ShapeDtypeStruct((16, 4, 32, DH), jnp.bfloat16),
        in_specs=[VM] * 7,
        out_specs=VM,
        compiler_params=PARAMS,
        name="add_up",
    )(dk, dv, *came, near, far)


def unpack_kernel(src_ref, *outs):
    for n, out in enumerate(outs):
        for h in range(16):
            out[:, h * DH:(h + 1) * DH] = src_ref[h, n]


def unpack(a):
    rows = jax.ShapeDtypeStruct((32, 16 * DH), jnp.bfloat16)
    return pl.pallas_call(
        unpack_kernel,
        out_shape=(rows,) * 4,
        in_specs=[VM],
        out_specs=(VM,) * 4,
        compiler_params=PARAMS,
        name="unpack",
    )(a)


def solution(mesh):
    grid = jax.sharding.Mesh(mesh.devices.reshape(8, 2, 4, 2, 2), ("z", "core", "x", "y1", "y0"))
    rows = P(("x", "y1", "y0", "z", "core"), None)
    return jax.shard_map(
        per_device,
        mesh=grid,
        in_specs=(rows, rows, rows, rows, P(), P()),
        out_specs=(rows,) * 4,
        check_vma=False,
    )
```

```python
import math

import jax
import jax.numpy as jnp
from jax import lax
from jax.experimental import pallas as pl
from jax.experimental.pallas import tpu as pltpu
from jax.sharding import PartitionSpec as P
from jax.sharding import PartitionSpec as P

DH = 128
TILE = 128
SCALE = 1.0 / math.sqrt(DH)
LOG2E = math.log2(math.e)
C1 = SCALE * LOG2E
QB = 256
KC = 512
NEG = -1e30
SHIFTS = (1, 3, 2)
BACK = (0, 1, 3, 2)
HALF = TILE // 2
NEAR, FAR = (0, 3), (1, 2)

NT = (((1,), (1,)), ((), ()))
NN = (((1,), (0,)), ((), ()))


def dot(a, b, dims):
    return lax.dot_general(a, b, dims, preferred_element_type=jnp.float32)


def load_rows(place, qg, n, rows5_s):
    for j in range(4):
        rows5_s[place[0] ^ (j // 2), :, place[1] ^ (j % 2)] = qg[j][:, n]


def stats_kernel(*refs):
    second = len(refs) == 15
    if second:
        q5_ref, g5_ref, kv, bias_ref, near_ref, near_out_ref = *refs[0:2], refs[2:4], *refs[4:7]
        stat_ref, out_ref, e_ref, part_ref = refs[7:11]
    else:
        place, qg, kv, bias_ref = refs[0], refs[1:5], refs[5:7], refs[7]
        stat_ref, out_ref, e_ref, q5_ref, g5_ref = refs[8:13]
        load_rows(place, qg, 0, q5_ref)
        load_rows(place, qg, 1, g5_ref)
    q_s, g_s = q5_ref.reshape(2048, DH), g5_ref.reshape(2048, DH)
    k_s, vt_s, xa_s, xb_s = refs[-4:]
    for j in range(2):
        rows = slice(j * KC, (j + 1) * KC)
        k_s[rows] = kv[j][:, 0].reshape(KC, DH)
        vt_s[:, rows] = kv[j][:, 1].reshape(KC, DH).T

    def score(qb, x_s):
        start = pl.multiple_of(qb * QB, QB)
        q = q_s[pl.ds(start, QB)]
        top = jnp.full((1, QB), NEG, jnp.float32)
        for c in range(2):
            s = dot(k_s[c * KC:(c + 1) * KC], q, NT) * C1
            bias = bias_ref[c * 8:(c + 1) * 8, pl.ds(start, QB)]
            x = (s.reshape(8, HALF, QB) + bias[:, None, :]).reshape(KC, QB)
            x_s[c * KC:(c + 1) * KC] = x
            top = jnp.maximum(top, jnp.max(x, axis=0, keepdims=True))
        return top

    def finish(qb, x_s, top):
        start = pl.multiple_of(qb * QB, QB)
        mass = jnp.zeros((1, QB), jnp.float32)
        acc = jnp.zeros((DH, QB), jnp.float32)
        for c in range(2):
            rows = slice(c * KC, (c + 1) * KC)
            e = jnp.exp2(x_s[rows] - top)
            mass = mass + jnp.sum(e, axis=0, keepdims=True)
            low = e.astype(jnp.bfloat16)
            e_ref[rows, pl.ds(start, QB)] = low
            acc = acc + dot(vt_s[:, rows], low, NN)
        if second:
            near_top = near_ref[0, pl.ds(qb, 1)]
            new_top = jnp.maximum(near_top, top)
            fades = jnp.exp2(near_top - new_top), jnp.exp2(top - new_top)
            acc = near_out_ref[:, pl.ds(start, QB)] * fades[0] + acc * fades[1]
            mass = near_ref[1, pl.ds(qb, 1)] * fades[0] + mass * fades[1]
            gt = g_s[pl.ds(start, QB)].astype(jnp.float32).T
            stat_ref[2, pl.ds(qb, 1)] = jnp.sum(gt * acc, axis=0, keepdims=True)
            part_ref[0, pl.ds(qb, 1)] = fades[0]
            part_ref[1, pl.ds(qb, 1)] = fades[1]
            top = new_top
        stat_ref[0, pl.ds(qb, 1)] = top
        stat_ref[1, pl.ds(qb, 1)] = mass
        out_ref[:, pl.ds(start, QB)] = acc

    def pair(i, top):
        top_b = score(2 * i + 1, xb_s)
        finish(2 * i, xa_s, top)
        top_a = score(jnp.minimum(2 * i + 2, 7), xa_s)
        finish(2 * i + 1, xb_s, top_b)
        return top_a

    lax.fori_loop(0, 4, pair, score(0, xa_s), unroll=2)


def grad_kernel(*refs):
    place, kv, q5_ref, g5_ref = refs[0], refs[1:5], *refs[5:7]
    e_refs, part_ref, acc_ref = refs[7:9], refs[9], refs[10]
    stats = refs[11:15]
    keep_ref, send_ref, dk_ref, dv_ref = refs[15:19]
    o5_s, dq5_s, kt_s, dk_s, dv_s, delta_s, fade_s = refs[19:26]
    q_s, g_s = q5_ref.reshape(2048, DH), g5_ref.reshape(2048, DH)
    o_s, dq_s = o5_s.reshape(2048, DH), dq5_s.reshape(2048, DH)
    for j in range(4):
        kt_s[:, j * KC:(j + 1) * KC] = kv[j][:, 0].reshape(KC, DH).T
    tops, masses, deltas = [[s[n] for s in stats] for n in range(3)]
    top = jnp.maximum(jnp.maximum(tops[0], tops[1]), jnp.maximum(tops[2], tops[3]))
    fades = [jnp.exp2(t - top) for t in tops]
    mass = sum(m * f for m, f in zip(masses, fades))
    inv_mass = 1.0 / mass
    delta_s[...] = sum(d * f for d, f in zip(deltas, fades)) * inv_mass
    fade_s[...] = fades[0] * inv_mass
    dk_s[...] = jnp.zeros_like(dk_s)
    dv_s[...] = jnp.zeros_like(dv_s)

    def block(qb):
        cols = slice(qb * QB, (qb + 1) * QB)
        q, g = q_s[cols], g_s[cols]
        gt = g.astype(jnp.float32).T
        delta, fade = delta_s[qb:qb + 1], fade_s[qb:qb + 1]
        o_s[cols] = (acc_ref[:, cols] * fade).T.astype(jnp.bfloat16)
        dqt = jnp.zeros((DH, QB), jnp.float32)
        for n, c in enumerate(NEAR + FAR):
            rows = slice(c * KC, (c + 1) * KC)
            half = slice(n % 2 * KC, (n % 2 + 1) * KC)
            if n % 2 == 0:
                local = fade * part_ref[n // 2, qb:qb + 1]
                gf = (gt * local).T.astype(jnp.bfloat16)
            e = e_refs[n // 2][half, cols]
            dp = dot(kv[c][:, 1].reshape(KC, DH), g, NT)
            ds = (e.astype(jnp.float32) * ((dp - delta) * local)).astype(jnp.bfloat16)
            dv_s[rows] += dot(e, gf, NN)
            dk_s[rows] += dot(ds, q, NN)
            dqt = dqt + dot(kt_s[:, rows], ds, NN)
        dq_s[cols] = (dqt * SCALE).T.astype(jnp.bfloat16)

    for qb in range(8):
        block(qb)
    for n, rows5 in enumerate((o5_s, dq5_s)):
        for far in range(2):
            keep_ref[n, far] = rows5[place[0] ^ far, :, place[1]]
            send_ref[n, far] = rows5[place[0] ^ far, :, 1 - place[1]]
    dk_ref[...] = (dk_s[...] * SCALE).astype(jnp.bfloat16)
    dv_ref[...] = dv_s[...].astype(jnp.bfloat16)


VM = pl.BlockSpec(memory_space=pltpu.VMEM)
SM = pl.BlockSpec(memory_space=pltpu.SMEM)
PARAMS = pltpu.CompilerParams(vmem_limit_bytes=16 * 1024 * 1024)
ROWS5 = pltpu.VMEM((2, 16, 2, 32, DH), jnp.bfloat16)


def cost(products):
    return pl.CostEstimate(
        flops=products * 2 * 2048 * 2048 * DH, bytes_accessed=1 << 22, transcendentals=1 << 21
    )


def run_stats(rows, kv, bias, *before):
    out_shape = [
        jax.ShapeDtypeStruct((3, 8, QB), jnp.float32),
        jax.ShapeDtypeStruct((DH, 2048), jnp.float32),
        jax.ShapeDtypeStruct((1024, 2048), jnp.bfloat16),
    ]
    if before:
        out_shape.append(jax.ShapeDtypeStruct((2, 8, QB), jnp.float32))
    else:
        out_shape += [jax.ShapeDtypeStruct((2, 16, 2, 32, DH), jnp.bfloat16)] * 2
    return pl.pallas_call(
        stats_kernel,
        out_shape=out_shape,
        in_specs=[VM] * 7 if before else [SM] + [VM] * 7,
        out_specs=[VM] * len(out_shape),
        scratch_shapes=[
            pltpu.VMEM((1024, DH), jnp.bfloat16),
            pltpu.VMEM((DH, 1024), jnp.bfloat16),
            pltpu.VMEM((1024, QB), jnp.float32),
            pltpu.VMEM((1024, QB), jnp.float32),
        ],
        compiler_params=PARAMS,
        cost_estimate=cost(1),
        name="stats_far" if before else "stats_near",
    )(*rows, *kv, bias, *before)


def run_grads(place, rows, kv, e, part, acc, stats):
    side = jax.ShapeDtypeStruct((2, 2, 16, 32, DH), jnp.bfloat16)
    keys = jax.ShapeDtypeStruct((2048, DH), jnp.bfloat16)
    return pl.pallas_call(
        grad_kernel,
        out_shape=(side, side, keys, keys),
        in_specs=[SM] + [VM] * 14,
        out_specs=(VM,) * 4,
        scratch_shapes=[ROWS5] * 2
        + [pltpu.VMEM((DH, 2048), jnp.bfloat16)]
        + [pltpu.VMEM((2048, DH), jnp.float32)] * 2
        + [pltpu.VMEM((8, QB), jnp.float32)] * 2,
        compiler_params=PARAMS,
        cost_estimate=cost(4),
        name="grads",
    )(place, *kv, *rows, *e, part, acc, *stats)


def ring(n, k):
    return [(i, (i + k) % n) for i in range(n)]


SWAP = [(0, 1), (1, 0)]
HEADS = ("y0", "z")


def per_device(queries, key_vectors, value_vectors, out_grad, key_tiles, tile_count):
    x_at, y1_at, core_at = [lax.axis_index(a) for a in ("x", "y1", "core")]
    head_at = lax.axis_index("y0") * 8 + lax.axis_index("z")
    place = jnp.stack([y1_at, core_at]).astype(jnp.int32)

    back = jnp.array([BACK[j] for j in NEAR + FAR], jnp.int32)
    tiles = jnp.arange(16, dtype=jnp.int32)
    k_tiles = (((x_at - back) % 4)[:, None] * 16 + y1_at * 8 + tiles[None, :8]).reshape(32)
    slots = key_tiles.shape[2]
    lists = lax.dynamic_slice(key_tiles, (head_at, x_at * 16, 0), (1, 16, slots))[0]
    counts = lax.dynamic_slice(tile_count, (head_at, x_at * 16), (1, 16))[0]
    live = jnp.arange(slots, dtype=jnp.int32)[None, :] < counts[:, None]
    lists = jnp.where(live, lists, -1)
    hit = jnp.any(lists[None, :, :] == k_tiles[:, None, None], axis=2)
    bias = jnp.repeat(jnp.where(hit, 0.0, NEG).astype(jnp.float32), TILE, axis=1)

    packed = pack(queries, out_grad, key_vectors, value_vectors)
    got = lax.all_to_all(packed, HEADS, split_axis=0, concat_axis=0, tiled=True)
    got, bias = lax.optimization_barrier((got, bias))
    qg_own, kv_own = got[:, 0:2], got[:, 2:4]
    kv = [kv_own] + [lax.ppermute(kv_own, "x", ring(4, k)) for k in SHIFTS]
    qg_far = lax.ppermute(qg_own, "y1", SWAP)
    qg = [
        qg_own,
        lax.ppermute(qg_own, "core", SWAP),
        qg_far,
        lax.ppermute(qg_far, "core", SWAP),
    ]
    near, near_acc, e_near, *full = run_stats(
        [place, *qg], [kv[j] for j in NEAR], bias[:16]
    )
    stat, acc, e_far, part = run_stats(
        full, [kv[j] for j in FAR], bias[16:], near, near_acc
    )
    stats = [
        stat,
        lax.ppermute(stat, "core", SWAP),
        lax.ppermute(stat, "y1", SWAP),
        lax.ppermute(stat, ("core", "y1"), [(i, 3 - i) for i in range(4)]),
    ]
    keep, away, dk, dv = run_grads(place, full, kv, (e_near, e_far), part, acc, stats)

    def pair(a, b, j):
        rows = slice(512 * j, 512 * (j + 1))
        return jnp.stack([a[rows], b[rows]])

    came = [lax.ppermute(pair(dk, dv, j), "x", ring(4, -BACK[j])) for j in (3, 1, 2)]
    near, far = add_core(keep, lax.ppermute(away, "core", SWAP))
    send = add_up(dk, dv, came, near, lax.ppermute(far, "y1", SWAP))
    back_home = lax.all_to_all(send, HEADS, split_axis=0, concat_axis=0, tiled=True)
    return unpack(back_home)


def add_core_kernel(keep_ref, came_ref, near_ref, far_ref):
    for n in range(2):
        for far, out in enumerate((near_ref, far_ref)):
            total = keep_ref[n, far].astype(jnp.float32) + came_ref[n, far].astype(jnp.float32)
            out[n] = total.astype(out.dtype)


def add_core(keep, came):
    return pl.pallas_call(
        add_core_kernel,
        out_shape=(
            jax.ShapeDtypeStruct((2, 16, 32, DH), jnp.float32),
            jax.ShapeDtypeStruct((2, 16, 32, DH), jnp.bfloat16),
        ),
        in_specs=[VM] * 2,
        out_specs=(VM,) * 2,
        compiler_params=PARAMS,
        name="add_core",
    )(keep, came)


def add_kernel(dk_ref, dv_ref, *refs):
    came, near_ref, far_ref, send_ref = refs[0:3], refs[3], refs[4], refs[5]
    for n in range(2):
        rows = near_ref[n] + far_ref[n].astype(jnp.float32)
        send_ref[:, n] = rows.astype(jnp.bfloat16)
    for n, own in enumerate((dk_ref, dv_ref)):
        total = own[0:512].astype(jnp.float32)
        for part in came:
            total = total + part[n].astype(jnp.float32)
        send_ref[:, 2 + n] = total.astype(jnp.bfloat16).reshape(16, 32, DH)


def add_up(dk, dv, came, near, far):
    return pl.pallas_call(
        add_kernel,
        out_shape=jax.ShapeDtypeStruct((16, 4, 32, DH), jnp.bfloat16),
        in_specs=[VM] * 7,
        out_specs=VM,
        compiler_params=PARAMS,
        name="add_up",
    )(dk, dv, *came, near, far)


def pack_kernel(*refs):
    arrays, out_ref, held, sems = refs[0:4], refs[4], refs[5], refs[6]
    copies = [pltpu.make_async_copy(arrays[n], held.at[n], sems.at[n]) for n in range(4)]
    for copy in copies:
        copy.start()
    for n, copy in enumerate(copies):
        copy.wait()
        for h in range(16):
            out_ref[h, n] = held[n, :, h * DH:(h + 1) * DH]


def pack(*arrays):
    return pl.pallas_call(
        pack_kernel,
        out_shape=jax.ShapeDtypeStruct((16, 4, 32, DH), jnp.bfloat16),
        in_specs=[pl.BlockSpec(memory_space=pl.ANY)] * 4,
        out_specs=VM,
        scratch_shapes=[
            pltpu.VMEM((4, 32, 16 * DH), jnp.bfloat16),
            pltpu.SemaphoreType.DMA((4,)),
        ],
        compiler_params=pltpu.CompilerParams(vmem_limit_bytes=60 * 1024 * 1024),
        name="pack",
    )(*arrays)


def unpack_kernel(src_ref, *outs):
    for n, out in enumerate(outs):
        for h in range(16):
            out[:, h * DH:(h + 1) * DH] = src_ref[h, n]


def unpack(a):
    rows = jax.ShapeDtypeStruct((32, 16 * DH), jnp.bfloat16)
    return pl.pallas_call(
        unpack_kernel,
        out_shape=(rows,) * 4,
        in_specs=[VM],
        out_specs=(VM,) * 4,
        compiler_params=PARAMS,
        name="unpack",
    )(a)


def solution(mesh):
    grid = jax.sharding.Mesh(mesh.devices.reshape(8, 2, 4, 2, 2), ("z", "core", "x", "y1", "y0"))
    rows = P(("x", "y1", "y0", "z", "core"), None)
    return jax.shard_map(
        per_device,
        mesh=grid,
        in_specs=(rows, rows, rows, rows, P(), P()),
        out_specs=(rows,) * 4,
        check_vma=False,
    )
```

```python
import math

import jax
import jax.numpy as jnp
from jax import lax
from jax.experimental import pallas as pl
from jax.experimental.pallas import tpu as pltpu
from jax.sharding import PartitionSpec as P
from jax.sharding import PartitionSpec as P

DH = 128
TILE = 128
SCALE = 1.0 / math.sqrt(DH)
LOG2E = math.log2(math.e)
C1 = SCALE * LOG2E
QB = 256
KC = 512
NEG = -1e30
HALF = TILE // 2
NEAR, FAR = (0, 3), (1, 2)
AWAY = (0, 3, 1, 2)

NT = (((1,), (1,)), ((), ()))
NN = (((1,), (0,)), ((), ()))


def dot(a, b, dims):
    return lax.dot_general(a, b, dims, preferred_element_type=jnp.float32)


def load_rows(place, qg, n, rows5_s):
    for j in range(4):
        rows5_s[place[0] ^ (j // 2), :, place[1] ^ (j % 2)] = qg[j][:, n]


def stats_kernel(*refs):
    second = len(refs) == 15
    if second:
        q5_ref, g5_ref, kv, bias_ref, near_ref, near_out_ref = *refs[0:2], refs[2:4], *refs[4:7]
        stat_ref, out_ref, e_ref, part_ref = refs[7:11]
    else:
        place, qg, kv, bias_ref = refs[0], refs[1:5], refs[5:7], refs[7]
        stat_ref, out_ref, e_ref, q5_ref, g5_ref = refs[8:13]
        load_rows(place, qg, 0, q5_ref)
        load_rows(place, qg, 1, g5_ref)
    q_s, g_s = q5_ref.reshape(2048, DH), g5_ref.reshape(2048, DH)
    k_s, vt_s, xa_s, xb_s = refs[-4:]
    for j in range(2):
        rows = slice(j * KC, (j + 1) * KC)
        k_s[rows] = kv[j][:, 0].reshape(KC, DH)
        vt_s[:DH, rows] = kv[j][:, 1].reshape(KC, DH).T
    vt_s[DH:] = jnp.ones((16, vt_s.shape[1]), jnp.bfloat16)

    def score(qb, x_s):
        start = pl.multiple_of(qb * QB, QB)
        q = q_s[pl.ds(start, QB)]
        top = jnp.full((1, QB), NEG, jnp.float32)
        for c in range(2):
            s = dot(k_s[c * KC:(c + 1) * KC], q, NT)
            x_s[c * KC:(c + 1) * KC] = s
            highs = jnp.max(s.reshape(8, HALF, QB), axis=1) * C1
            highs = highs + bias_ref[c * 8:(c + 1) * 8, pl.ds(start, QB)]
            top = jnp.maximum(top, jnp.max(highs, axis=0, keepdims=True))
        return top

    def finish(qb, x_s, top):
        start = pl.multiple_of(qb * QB, QB)
        acc = jnp.zeros((DH + 16, QB), jnp.float32)
        for c in range(2):
            rows = slice(c * KC, (c + 1) * KC)
            shift = bias_ref[c * 8:(c + 1) * 8, pl.ds(start, QB)] - jnp.maximum(top, NEG / 2)
            x = x_s[rows].reshape(8, HALF, QB) * C1 + shift[:, None, :]
            low = jnp.exp2(x).reshape(KC, QB).astype(jnp.bfloat16)
            e_ref[rows, pl.ds(start, QB)] = low
            acc = acc + dot(vt_s[:, rows], low, NN)
        acc, mass = acc[:DH], acc[DH:DH + 1]
        if second:
            near_top = near_ref[0, pl.ds(qb, 1)]
            new_top = jnp.maximum(near_top, top)
            fades = jnp.exp2(near_top - new_top), jnp.exp2(top - new_top)
            acc = near_out_ref[:, pl.ds(start, QB)] * fades[0] + acc * fades[1]
            mass = near_ref[1, pl.ds(qb, 1)] * fades[0] + mass * fades[1]
            gt = g_s[pl.ds(start, QB)].astype(jnp.float32).T
            stat_ref[2, pl.ds(qb, 1)] = jnp.sum(gt * acc, axis=0, keepdims=True)
            part_ref[0, pl.ds(qb, 1)] = fades[0]
            part_ref[1, pl.ds(qb, 1)] = fades[1]
            top = new_top
        stat_ref[0, pl.ds(qb, 1)] = top
        stat_ref[1, pl.ds(qb, 1)] = mass
        out_ref[:, pl.ds(start, QB)] = acc

    def pair(i, top):
        top_b = score(2 * i + 1, xb_s)
        finish(2 * i, xa_s, top)
        top_a = score(jnp.minimum(2 * i + 2, 7), xa_s)
        finish(2 * i + 1, xb_s, top_b)
        return top_a

    lax.fori_loop(0, 4, pair, score(0, xa_s), unroll=2)


def grad_kernel(*refs):
    place, kv, q5_ref, g5_ref = refs[0], refs[1:5], *refs[5:7]
    e_refs, part_ref, acc_ref = refs[7:9], refs[9], refs[10]
    stats = refs[11:15]
    keep_ref, send_ref, dk_ref, dv_ref = refs[15:19]
    o5_s, dq5_s, kt_s, dk_s, dv_s, delta_s, fade_s = refs[19:26]
    q_s, g_s = q5_ref.reshape(2048, DH), g5_ref.reshape(2048, DH)
    o_s, dq_s = o5_s.reshape(2048, DH), dq5_s.reshape(2048, DH)
    for j in range(4):
        kt_s[:, j * KC:(j + 1) * KC] = kv[j][:, 0].reshape(KC, DH).T
    tops, masses, deltas = [[s[n] for s in stats] for n in range(3)]
    top = jnp.maximum(jnp.maximum(tops[0], tops[1]), jnp.maximum(tops[2], tops[3]))
    fades = [jnp.exp2(t - top) for t in tops]
    mass = sum(m * f for m, f in zip(masses, fades))
    inv_mass = 1.0 / mass
    delta_s[...] = sum(d * f for d, f in zip(deltas, fades)) * inv_mass
    fade_s[...] = fades[0] * inv_mass
    dk_s[...] = jnp.zeros_like(dk_s)
    dv_s[...] = jnp.zeros_like(dv_s)

    def block(qb):
        cols = slice(qb * QB, (qb + 1) * QB)
        q, g = q_s[cols], g_s[cols]
        gt = g.astype(jnp.float32).T
        delta, fade = delta_s[qb:qb + 1], fade_s[qb:qb + 1]
        o_s[cols] = (acc_ref[:, cols] * fade).T.astype(jnp.bfloat16)
        dqt = jnp.zeros((DH, QB), jnp.float32)
        for n, c in enumerate(NEAR + FAR):
            rows = slice(c * KC, (c + 1) * KC)
            half = slice(n % 2 * KC, (n % 2 + 1) * KC)
            if n % 2 == 0:
                local = fade * part_ref[n // 2, qb:qb + 1]
                gf = (gt * local).T.astype(jnp.bfloat16)
            e = e_refs[n // 2][half, cols]
            dp = dot(kv[c][:, 1].reshape(KC, DH), g, NT)
            ds = (e.astype(jnp.float32) * ((dp - delta) * local)).astype(jnp.bfloat16)
            dv_s[rows] += dot(e, gf, NN)
            dk_s[rows] += dot(ds, q, NN)
            dqt = dqt + dot(kt_s[:, rows], ds, NN)
        dq_s[cols] = (dqt * SCALE).T.astype(jnp.bfloat16)

    for qb in range(8):
        block(qb)
    for n, rows5 in enumerate((o5_s, dq5_s)):
        for far in range(2):
            keep_ref[n, far] = rows5[place[0] ^ far, :, place[1]]
            send_ref[n, far] = rows5[place[0] ^ far, :, 1 - place[1]]
    dk_ref[...] = (dk_s[...] * SCALE).astype(jnp.bfloat16)
    dv_ref[...] = dv_s[...].astype(jnp.bfloat16)


VM = pl.BlockSpec(memory_space=pltpu.VMEM)
SM = pl.BlockSpec(memory_space=pltpu.SMEM)
PARAMS = pltpu.CompilerParams(vmem_limit_bytes=16 * 1024 * 1024)
ROWS5 = pltpu.VMEM((2, 16, 2, 32, DH), jnp.bfloat16)


def cost(products):
    return pl.CostEstimate(
        flops=products * 2 * 2048 * 2048 * DH, bytes_accessed=1 << 22, transcendentals=1 << 21
    )


def run_stats(rows, kv, bias, *before):
    out_shape = [
        jax.ShapeDtypeStruct((3, 8, QB), jnp.float32),
        jax.ShapeDtypeStruct((DH, 2048), jnp.float32),
        jax.ShapeDtypeStruct((1024, 2048), jnp.bfloat16),
    ]
    if before:
        out_shape.append(jax.ShapeDtypeStruct((2, 8, QB), jnp.float32))
    else:
        out_shape += [jax.ShapeDtypeStruct((2, 16, 2, 32, DH), jnp.bfloat16)] * 2
    return pl.pallas_call(
        stats_kernel,
        out_shape=out_shape,
        in_specs=[VM] * 7 if before else [SM] + [VM] * 7,
        out_specs=[VM] * len(out_shape),
        scratch_shapes=[
            pltpu.VMEM((1024, DH), jnp.bfloat16),
            pltpu.VMEM((DH + 16, 1024), jnp.bfloat16),
            pltpu.VMEM((1024, QB), jnp.float32),
            pltpu.VMEM((1024, QB), jnp.float32),
        ],
        compiler_params=PARAMS,
        cost_estimate=cost(1),
        name="stats_far" if before else "stats_near",
    )(*rows, *kv, bias, *before)


def run_grads(place, rows, kv, e, part, acc, stats):
    side = jax.ShapeDtypeStruct((2, 2, 16, 32, DH), jnp.bfloat16)
    keys = jax.ShapeDtypeStruct((2048, DH), jnp.bfloat16)
    return pl.pallas_call(
        grad_kernel,
        out_shape=(side, side, keys, keys),
        in_specs=[SM] + [VM] * 14,
        out_specs=(VM,) * 4,
        scratch_shapes=[ROWS5] * 2
        + [pltpu.VMEM((DH, 2048), jnp.bfloat16)]
        + [pltpu.VMEM((2048, DH), jnp.float32)] * 2
        + [pltpu.VMEM((8, QB), jnp.float32)] * 2,
        compiler_params=PARAMS,
        cost_estimate=cost(4),
        name="grads",
    )(place, *kv, *rows, *e, part, acc, *stats)


def swap(a, j):
    return lax.ppermute(a, "x", [(i, i ^ j) for i in range(4)])


SWAP = [(0, 1), (1, 0)]
HEADS = ("y0", "z")


def per_device(queries, key_vectors, value_vectors, out_grad, key_tiles, tile_count):
    x_at, y1_at, core_at = [lax.axis_index(a) for a in ("x", "y1", "core")]
    head_at = lax.axis_index("y0") * 8 + lax.axis_index("z")
    place = jnp.stack([y1_at, core_at]).astype(jnp.int32)

    away = jnp.array([AWAY[j] for j in NEAR + FAR], jnp.int32)
    tiles = jnp.arange(16, dtype=jnp.int32)
    k_tiles = ((x_at ^ away)[:, None] * 16 + y1_at * 8 + tiles[None, :8]).reshape(32)
    slots = key_tiles.shape[2]
    lists = lax.dynamic_slice(key_tiles, (head_at, x_at * 16, 0), (1, 16, slots))[0]
    counts = lax.dynamic_slice(tile_count, (head_at, x_at * 16), (1, 16))[0]
    live = jnp.arange(slots, dtype=jnp.int32)[None, :] < counts[:, None]
    lists = jnp.where(live, lists, -1)
    hit = jnp.any(lists[None, :, :] == k_tiles[:, None, None], axis=2)
    bias = jnp.repeat(jnp.where(hit, 0.0, NEG).astype(jnp.float32), TILE, axis=1)

    packed = pack(queries, out_grad, key_vectors, value_vectors)
    got = lax.all_to_all(packed, HEADS, split_axis=0, concat_axis=0, tiled=True)
    got, bias = lax.optimization_barrier((got, bias))
    qg_own, kv_own = got[:, 0:2], got[:, 2:4]
    kv = [kv_own] + [swap(kv_own, j) for j in AWAY[1:]]
    qg_far = lax.ppermute(qg_own, "y1", SWAP)
    qg = [
        qg_own,
        lax.ppermute(qg_own, "core", SWAP),
        qg_far,
        lax.ppermute(qg_far, "core", SWAP),
    ]
    near, near_acc, e_near, *full = run_stats(
        [place, *qg], [kv[j] for j in NEAR], bias[:16]
    )
    stat, acc, e_far, part = run_stats(
        full, [kv[j] for j in FAR], bias[16:], near, near_acc
    )
    stats = [
        stat,
        lax.ppermute(stat, "core", SWAP),
        lax.ppermute(stat, "y1", SWAP),
        lax.ppermute(stat, ("core", "y1"), [(i, 3 - i) for i in range(4)]),
    ]
    keep, leave, dk, dv = run_grads(place, full, kv, (e_near, e_far), part, acc, stats)

    def pair(a, b, j):
        rows = slice(512 * j, 512 * (j + 1))
        return jnp.stack([a[rows], b[rows]])

    came = [swap(pair(dk, dv, j), AWAY[j]) for j in (3, 2, 1)]
    near, far = add_core(keep, lax.ppermute(leave, "core", SWAP))
    send = add_up(dk, dv, came, near, lax.ppermute(far, "y1", SWAP))
    back_home = lax.all_to_all(send, HEADS, split_axis=0, concat_axis=0, tiled=True)
    return unpack(back_home)


def add_core_kernel(keep_ref, came_ref, near_ref, far_ref):
    for n in range(2):
        for far, out in enumerate((near_ref, far_ref)):
            total = keep_ref[n, far].astype(jnp.float32) + came_ref[n, far].astype(jnp.float32)
            out[n] = total.astype(out.dtype)


def add_core(keep, came):
    return pl.pallas_call(
        add_core_kernel,
        out_shape=(
            jax.ShapeDtypeStruct((2, 16, 32, DH), jnp.float32),
            jax.ShapeDtypeStruct((2, 16, 32, DH), jnp.bfloat16),
        ),
        in_specs=[VM] * 2,
        out_specs=(VM,) * 2,
        compiler_params=PARAMS,
        name="add_core",
    )(keep, came)


def add_kernel(dk_ref, dv_ref, *refs):
    came, near_ref, far_ref, send_ref = refs[0:3], refs[3], refs[4], refs[5]
    for n in range(2):
        rows = near_ref[n] + far_ref[n].astype(jnp.float32)
        send_ref[:, n] = rows.astype(jnp.bfloat16)
    for n, own in enumerate((dk_ref, dv_ref)):
        total = own[0:512].astype(jnp.float32)
        for part in came:
            total = total + part[n].astype(jnp.float32)
        send_ref[:, 2 + n] = total.astype(jnp.bfloat16).reshape(16, 32, DH)


def add_up(dk, dv, came, near, far):
    return pl.pallas_call(
        add_kernel,
        out_shape=jax.ShapeDtypeStruct((16, 4, 32, DH), jnp.bfloat16),
        in_specs=[VM] * 7,
        out_specs=VM,
        compiler_params=PARAMS,
        name="add_up",
    )(dk, dv, *came, near, far)


def pack_kernel(*refs):
    arrays, out_ref, held, sems = refs[0:4], refs[4], refs[5], refs[6]
    copies = [pltpu.make_async_copy(arrays[n], held.at[n], sems.at[n]) for n in range(4)]
    for copy in copies:
        copy.start()
    for n, copy in enumerate(copies):
        copy.wait()
        for h in range(16):
            out_ref[h, n] = held[n, :, h * DH:(h + 1) * DH]


def pack(*arrays):
    return pl.pallas_call(
        pack_kernel,
        out_shape=jax.ShapeDtypeStruct((16, 4, 32, DH), jnp.bfloat16),
        in_specs=[pl.BlockSpec(memory_space=pl.ANY)] * 4,
        out_specs=VM,
        scratch_shapes=[
            pltpu.VMEM((4, 32, 16 * DH), jnp.bfloat16),
            pltpu.SemaphoreType.DMA((4,)),
        ],
        compiler_params=pltpu.CompilerParams(vmem_limit_bytes=60 * 1024 * 1024),
        name="pack",
    )(*arrays)


def unpack_kernel(src_ref, *outs):
    for n, out in enumerate(outs):
        for h in range(16):
            out[:, h * DH:(h + 1) * DH] = src_ref[h, n]


def unpack(a):
    rows = jax.ShapeDtypeStruct((32, 16 * DH), jnp.bfloat16)
    return pl.pallas_call(
        unpack_kernel,
        out_shape=(rows,) * 4,
        in_specs=[VM],
        out_specs=(VM,) * 4,
        compiler_params=PARAMS,
        name="unpack",
    )(a)


def solution(mesh):
    grid = jax.sharding.Mesh(mesh.devices.reshape(8, 2, 4, 2, 2), ("z", "core", "x", "y1", "y0"))
    rows = P(("x", "y1", "y0", "z", "core"), None)
    return jax.shard_map(
        per_device,
        mesh=grid,
        in_specs=(rows, rows, rows, rows, P(), P()),
        out_specs=(rows,) * 4,
        check_vma=False,
    )
```

```python
import math

import jax
import jax.numpy as jnp
from jax import lax
from jax.experimental import pallas as pl
from jax.experimental.pallas import tpu as pltpu
from jax.sharding import PartitionSpec as P
from jax.sharding import PartitionSpec as P

DH = 128
TILE = 128
SCALE = 1.0 / math.sqrt(DH)
LOG2E = math.log2(math.e)
C1 = SCALE * LOG2E
QB = 256
KC = 512
NEG = -1e30
HALF = TILE // 2
NEAR, FAR = (0, 3), (1, 2)
AWAY = (0, 3, 1, 2)

NT = (((1,), (1,)), ((), ()))
NN = (((1,), (0,)), ((), ()))


def dot(a, b, dims):
    return lax.dot_general(a, b, dims, preferred_element_type=jnp.float32)


def load_rows(place, qg, n, rows5_s):
    for j in range(4):
        rows5_s[place[0] ^ (j // 2), :, place[1] ^ (j % 2)] = qg[j][:, n]


def stats_kernel(*refs):
    second = len(refs) == 15
    if second:
        q5_ref, g5_ref, kv, bias_ref, near_ref, near_out_ref = *refs[0:2], refs[2:4], *refs[4:7]
        stat_ref, out_ref, e_ref, part_ref = refs[7:11]
    else:
        place, qg, kv, bias_ref = refs[0], refs[1:5], refs[5:7], refs[7]
        stat_ref, out_ref, e_ref, q5_ref, g5_ref = refs[8:13]
        load_rows(place, qg, 0, q5_ref)
        load_rows(place, qg, 1, g5_ref)
    q_s, g_s = q5_ref.reshape(2048, DH), g5_ref.reshape(2048, DH)
    k_s, vt_s, xa_s, xb_s = refs[-4:]
    for j in range(2):
        rows = slice(j * KC, (j + 1) * KC)
        k_s[rows] = kv[j][:, 0].reshape(KC, DH)
        vt_s[:DH, rows] = kv[j][:, 1].reshape(KC, DH).T
    vt_s[DH:] = jnp.ones((16, vt_s.shape[1]), jnp.bfloat16)

    def score(qb, x_s):
        start = pl.multiple_of(qb * QB, QB)
        q = q_s[pl.ds(start, QB)]
        top = jnp.full((1, QB), NEG, jnp.float32)
        for c in range(2):
            s = dot(k_s[c * KC:(c + 1) * KC], q, NT)
            x_s[c * KC:(c + 1) * KC] = s
            highs = jnp.max(s.reshape(8, HALF, QB), axis=1) * C1
            highs = highs + bias_ref[c * 8:(c + 1) * 8, pl.ds(start, QB)]
            top = jnp.maximum(top, jnp.max(highs, axis=0, keepdims=True))
        return top

    def finish(qb, x_s, top):
        start = pl.multiple_of(qb * QB, QB)
        acc = jnp.zeros((DH + 16, QB), jnp.float32)
        for c in range(2):
            rows = slice(c * KC, (c + 1) * KC)
            shift = bias_ref[c * 8:(c + 1) * 8, pl.ds(start, QB)] - jnp.maximum(top, NEG / 2)
            x = x_s[rows].reshape(8, HALF, QB) * C1 + shift[:, None, :]
            low = jnp.exp2(x).reshape(KC, QB).astype(jnp.bfloat16)
            e_ref[rows, pl.ds(start, QB)] = low
            acc = acc + dot(vt_s[:, rows], low, NN)
        acc, mass = acc[:DH], acc[DH:DH + 1]
        if second:
            near_top = near_ref[0, pl.ds(qb, 1)]
            new_top = jnp.maximum(near_top, top)
            fades = jnp.exp2(near_top - new_top), jnp.exp2(top - new_top)
            acc = near_out_ref[:, pl.ds(start, QB)] * fades[0] + acc * fades[1]
            mass = near_ref[1, pl.ds(qb, 1)] * fades[0] + mass * fades[1]
            gt = g_s[pl.ds(start, QB)].astype(jnp.float32).T
            stat_ref[2, pl.ds(qb, 1)] = jnp.sum(gt * acc, axis=0, keepdims=True)
            part_ref[0, pl.ds(qb, 1)] = fades[0]
            part_ref[1, pl.ds(qb, 1)] = fades[1]
            top = new_top
        stat_ref[0, pl.ds(qb, 1)] = top
        stat_ref[1, pl.ds(qb, 1)] = mass
        out_ref[:, pl.ds(start, QB)] = acc

    def pair(i, top):
        top_b = score(2 * i + 1, xb_s)
        finish(2 * i, xa_s, top)
        top_a = score(jnp.minimum(2 * i + 2, 7), xa_s)
        finish(2 * i + 1, xb_s, top_b)
        return top_a

    lax.fori_loop(0, 4, pair, score(0, xa_s), unroll=4)


def grad_kernel(*refs):
    place, kv, q5_ref, g5_ref = refs[0], refs[1:5], *refs[5:7]
    e_refs, part_ref, acc_ref = refs[7:9], refs[9], refs[10]
    stats = refs[11:15]
    keep_ref, send_ref, dk_ref, dv_ref = refs[15:19]
    o5_s, dq5_s, kt_s, dk_s, dv_s, delta_s, fade_s = refs[19:26]
    q_s, g_s = q5_ref.reshape(2048, DH), g5_ref.reshape(2048, DH)
    o_s, dq_s = o5_s.reshape(2048, DH), dq5_s.reshape(2048, DH)
    for j in range(4):
        kt_s[:, j * KC:(j + 1) * KC] = kv[j][:, 0].reshape(KC, DH).T
    tops, masses, deltas = [[s[n] for s in stats] for n in range(3)]
    top = jnp.maximum(jnp.maximum(tops[0], tops[1]), jnp.maximum(tops[2], tops[3]))
    fades = [jnp.exp2(t - top) for t in tops]
    mass = sum(m * f for m, f in zip(masses, fades))
    inv_mass = 1.0 / mass
    delta_s[...] = sum(d * f for d, f in zip(deltas, fades)) * inv_mass
    fade_s[...] = fades[0] * inv_mass
    dk_s[...] = jnp.zeros_like(dk_s)
    dv_s[...] = jnp.zeros_like(dv_s)

    def block(qb):
        cols = slice(qb * QB, (qb + 1) * QB)
        q, g = q_s[cols], g_s[cols]
        gt = g.astype(jnp.float32).T
        delta, fade = delta_s[qb:qb + 1], fade_s[qb:qb + 1]
        o_s[cols] = (acc_ref[:, cols] * fade).T.astype(jnp.bfloat16)
        dqt = jnp.zeros((DH, QB), jnp.float32)
        for n, c in enumerate(NEAR + FAR):
            rows = slice(c * KC, (c + 1) * KC)
            half = slice(n % 2 * KC, (n % 2 + 1) * KC)
            if n % 2 == 0:
                local = fade * part_ref[n // 2, qb:qb + 1]
                gf = (gt * local).T.astype(jnp.bfloat16)
            e = e_refs[n // 2][half, cols]
            dp = dot(kv[c][:, 1].reshape(KC, DH), g, NT)
            ds = (e.astype(jnp.float32) * ((dp - delta) * local)).astype(jnp.bfloat16)
            dv_s[rows] += dot(e, gf, NN)
            dk_s[rows] += dot(ds, q, NN)
            dqt = dqt + dot(kt_s[:, rows], ds, NN)
        dq_s[cols] = (dqt * SCALE).T.astype(jnp.bfloat16)

    for qb in range(8):
        block(qb)
    for n, rows5 in enumerate((o5_s, dq5_s)):
        for far in range(2):
            keep_ref[n, far] = rows5[place[0] ^ far, :, place[1]]
            send_ref[n, far] = rows5[place[0] ^ far, :, 1 - place[1]]
    dk_ref[...] = (dk_s[...] * SCALE).astype(jnp.bfloat16)
    dv_ref[...] = dv_s[...].astype(jnp.bfloat16)


VM = pl.BlockSpec(memory_space=pltpu.VMEM)
SM = pl.BlockSpec(memory_space=pltpu.SMEM)
PARAMS = pltpu.CompilerParams(vmem_limit_bytes=16 * 1024 * 1024)
ROWS5 = pltpu.VMEM((2, 16, 2, 32, DH), jnp.bfloat16)


def run_stats(rows, kv, bias, *before):
    out_shape = [
        jax.ShapeDtypeStruct((3, 8, QB), jnp.float32),
        jax.ShapeDtypeStruct((DH, 2048), jnp.float32),
        jax.ShapeDtypeStruct((1024, 2048), jnp.bfloat16),
    ]
    if before:
        out_shape.append(jax.ShapeDtypeStruct((2, 8, QB), jnp.float32))
    else:
        out_shape += [jax.ShapeDtypeStruct((2, 16, 2, 32, DH), jnp.bfloat16)] * 2
    return pl.pallas_call(
        stats_kernel,
        out_shape=out_shape,
        in_specs=[VM] * 7 if before else [SM] + [VM] * 7,
        out_specs=[VM] * len(out_shape),
        scratch_shapes=[
            pltpu.VMEM((1024, DH), jnp.bfloat16),
            pltpu.VMEM((DH + 16, 1024), jnp.bfloat16),
            pltpu.VMEM((1024, QB), jnp.float32),
            pltpu.VMEM((1024, QB), jnp.float32),
        ],
        compiler_params=PARAMS,
        name="stats_far" if before else "stats_near",
    )(*rows, *kv, bias, *before)


def run_grads(place, rows, kv, e, part, acc, stats):
    side = jax.ShapeDtypeStruct((2, 2, 16, 32, DH), jnp.bfloat16)
    keys = jax.ShapeDtypeStruct((2048, DH), jnp.bfloat16)
    return pl.pallas_call(
        grad_kernel,
        out_shape=(side, side, keys, keys),
        in_specs=[SM] + [VM] * 14,
        out_specs=(VM,) * 4,
        scratch_shapes=[ROWS5] * 2
        + [pltpu.VMEM((DH, 2048), jnp.bfloat16)]
        + [pltpu.VMEM((2048, DH), jnp.float32)] * 2
        + [pltpu.VMEM((8, QB), jnp.float32)] * 2,
        compiler_params=PARAMS,
        name="grads",
    )(place, *kv, *rows, *e, part, acc, *stats)


def swap(a, j):
    return lax.ppermute(a, "x", [(i, i ^ j) for i in range(4)])


SWAP = [(0, 1), (1, 0)]
HEADS = ("y0", "z")


def per_device(queries, key_vectors, value_vectors, out_grad, key_tiles, tile_count):
    x_at, y1_at, core_at = [lax.axis_index(a) for a in ("x", "y1", "core")]
    head_at = lax.axis_index("y0") * 8 + lax.axis_index("z")
    place = jnp.stack([y1_at, core_at]).astype(jnp.int32)

    away = jnp.array([AWAY[j] for j in NEAR + FAR], jnp.int32)
    tiles = jnp.arange(16, dtype=jnp.int32)
    k_tiles = ((x_at ^ away)[:, None] * 16 + y1_at * 8 + tiles[None, :8]).reshape(32)
    slots = key_tiles.shape[2]
    lists = lax.dynamic_slice(key_tiles, (head_at, x_at * 16, 0), (1, 16, slots))[0]
    counts = lax.dynamic_slice(tile_count, (head_at, x_at * 16), (1, 16))[0]
    live = jnp.arange(slots, dtype=jnp.int32)[None, :] < counts[:, None]
    lists = jnp.where(live, lists, -1)
    hit = jnp.any(lists[None, :, :] == k_tiles[:, None, None], axis=2)
    bias = jnp.repeat(jnp.where(hit, 0.0, NEG).astype(jnp.float32), TILE, axis=1)

    packed = pack(queries, out_grad, key_vectors, value_vectors)
    got = lax.all_to_all(packed, HEADS, split_axis=0, concat_axis=0, tiled=True)
    got, bias = lax.optimization_barrier((got, bias))
    qg_own, kv_own = got[:, 0:2], got[:, 2:4]
    kv = [kv_own] + [swap(kv_own, j) for j in AWAY[1:]]
    qg_far = lax.ppermute(qg_own, "y1", SWAP)
    qg = [
        qg_own,
        lax.ppermute(qg_own, "core", SWAP),
        qg_far,
        lax.ppermute(qg_far, "core", SWAP),
    ]
    near, near_acc, e_near, *full = run_stats(
        [place, *qg], [kv[j] for j in NEAR], bias[:16]
    )
    stat, acc, e_far, part = run_stats(
        full, [kv[j] for j in FAR], bias[16:], near, near_acc
    )
    stats = [
        stat,
        lax.ppermute(stat, "core", SWAP),
        lax.ppermute(stat, "y1", SWAP),
        lax.ppermute(stat, ("core", "y1"), [(i, 3 - i) for i in range(4)]),
    ]
    keep, leave, dk, dv = run_grads(place, full, kv, (e_near, e_far), part, acc, stats)

    def pair(a, b, j):
        rows = slice(512 * j, 512 * (j + 1))
        return jnp.stack([a[rows], b[rows]])

    came = [swap(pair(dk, dv, j), AWAY[j]) for j in (3, 2, 1)]
    near, far = add_core(keep, lax.ppermute(leave, "core", SWAP))
    send = add_up(dk, dv, came, near, lax.ppermute(far, "y1", SWAP))
    back_home = lax.all_to_all(send, HEADS, split_axis=0, concat_axis=0, tiled=True)
    return unpack(back_home)


def add_core_kernel(keep_ref, came_ref, near_ref, far_ref):
    for n in range(2):
        for far, out in enumerate((near_ref, far_ref)):
            total = keep_ref[n, far].astype(jnp.float32) + came_ref[n, far].astype(jnp.float32)
            out[n] = total.astype(out.dtype)


def add_core(keep, came):
    return pl.pallas_call(
        add_core_kernel,
        out_shape=(
            jax.ShapeDtypeStruct((2, 16, 32, DH), jnp.float32),
            jax.ShapeDtypeStruct((2, 16, 32, DH), jnp.bfloat16),
        ),
        in_specs=[VM] * 2,
        out_specs=(VM,) * 2,
        compiler_params=PARAMS,
        name="add_core",
    )(keep, came)


def add_kernel(dk_ref, dv_ref, *refs):
    came, near_ref, far_ref, send_ref = refs[0:3], refs[3], refs[4], refs[5]
    for n in range(2):
        rows = near_ref[n] + far_ref[n].astype(jnp.float32)
        send_ref[:, n] = rows.astype(jnp.bfloat16)
    for n, own in enumerate((dk_ref, dv_ref)):
        total = own[0:512].astype(jnp.float32)
        for part in came:
            total = total + part[n].astype(jnp.float32)
        send_ref[:, 2 + n] = total.astype(jnp.bfloat16).reshape(16, 32, DH)


def add_up(dk, dv, came, near, far):
    return pl.pallas_call(
        add_kernel,
        out_shape=jax.ShapeDtypeStruct((16, 4, 32, DH), jnp.bfloat16),
        in_specs=[VM] * 7,
        out_specs=VM,
        compiler_params=PARAMS,
        name="add_up",
    )(dk, dv, *came, near, far)


def pack_kernel(*refs):
    arrays, out_ref, held, sems = refs[0:4], refs[4], refs[5], refs[6]
    copies = [pltpu.make_async_copy(arrays[n], held.at[n], sems.at[n]) for n in range(4)]
    for copy in copies:
        copy.start()
    for n, copy in enumerate(copies):
        copy.wait()
        for h in range(16):
            out_ref[h, n] = held[n, :, h * DH:(h + 1) * DH]


def pack(*arrays):
    return pl.pallas_call(
        pack_kernel,
        out_shape=jax.ShapeDtypeStruct((16, 4, 32, DH), jnp.bfloat16),
        in_specs=[pl.BlockSpec(memory_space=pl.ANY)] * 4,
        out_specs=VM,
        scratch_shapes=[
            pltpu.VMEM((4, 32, 16 * DH), jnp.bfloat16),
            pltpu.SemaphoreType.DMA((4,)),
        ],
        compiler_params=pltpu.CompilerParams(vmem_limit_bytes=60 * 1024 * 1024),
        name="pack",
    )(*arrays)


def unpack_kernel(src_ref, *outs):
    for n, out in enumerate(outs):
        for h in range(16):
            out[:, h * DH:(h + 1) * DH] = src_ref[h, n]


def unpack(a):
    rows = jax.ShapeDtypeStruct((32, 16 * DH), jnp.bfloat16)
    return pl.pallas_call(
        unpack_kernel,
        out_shape=(rows,) * 4,
        in_specs=[VM],
        out_specs=(VM,) * 4,
        compiler_params=PARAMS,
        name="unpack",
    )(a)


def solution(mesh):
    grid = jax.sharding.Mesh(mesh.devices.reshape(8, 2, 4, 2, 2), ("z", "core", "x", "y1", "y0"))
    rows = P(("x", "y1", "y0", "z", "core"), None)
    return jax.shard_map(
        per_device,
        mesh=grid,
        in_specs=(rows, rows, rows, rows, P(), P()),
        out_specs=(rows,) * 4,
        check_vma=False,
    )
```

```python
import math

import jax
import jax.numpy as jnp
from jax import lax
from jax.experimental import pallas as pl
from jax.experimental.pallas import tpu as pltpu
from jax.sharding import PartitionSpec as P
from jax.sharding import PartitionSpec as P

DH = 128
TILE = 128
SCALE = 1.0 / math.sqrt(DH)
LOG2E = math.log2(math.e)
C1 = SCALE * LOG2E
QB = 256
KC = 512
NEG = -1e30
HALF = TILE // 2
NEAR, FAR = (0, 3), (1, 2)
AWAY = (0, 3, 1, 2)

NT = (((1,), (1,)), ((), ()))
NN = (((1,), (0,)), ((), ()))


def dot(a, b, dims):
    return lax.dot_general(a, b, dims, preferred_element_type=jnp.float32)


def load_rows(place, qg, n, rows5_s):
    for j in range(4):
        rows5_s[place[0] ^ (j // 2), :, place[1] ^ (j % 2)] = qg[j][:, n]


def stats_kernel(*refs):
    second = len(refs) == 15
    if second:
        q5_ref, g5_ref, kv, bias_ref, near_ref, near_out_ref = *refs[0:2], refs[2:4], *refs[4:7]
        stat_ref, out_ref, e_ref, part_ref = refs[7:11]
    else:
        place, qg, kv, bias_ref = refs[0], refs[1:5], refs[5:7], refs[7]
        stat_ref, out_ref, e_ref, q5_ref, g5_ref = refs[8:13]
        load_rows(place, qg, 0, q5_ref)
        load_rows(place, qg, 1, g5_ref)
    q_s, g_s = q5_ref.reshape(2048, DH), g5_ref.reshape(2048, DH)
    k_s, vt_s, xa_s, xb_s = refs[-4:]
    for j in range(2):
        rows = slice(j * KC, (j + 1) * KC)
        k_s[rows] = kv[j][:, 0].reshape(KC, DH)
        vt_s[:DH, rows] = kv[j][:, 1].reshape(KC, DH).T
    vt_s[DH:] = jnp.ones((16, vt_s.shape[1]), jnp.bfloat16)

    def score(qb, x_s):
        start = pl.multiple_of(qb * QB, QB)
        q = q_s[pl.ds(start, QB)]
        top = jnp.full((1, QB), NEG, jnp.float32)
        for c in range(2):
            s = dot(k_s[c * KC:(c + 1) * KC], q, NT)
            x_s[c * KC:(c + 1) * KC] = s
            highs = jnp.max(s.reshape(8, HALF, QB), axis=1) * C1
            highs = highs + bias_ref[c * 8:(c + 1) * 8, pl.ds(start, QB)]
            top = jnp.maximum(top, jnp.max(highs, axis=0, keepdims=True))
        return top

    def finish(qb, x_s, top):
        start = pl.multiple_of(qb * QB, QB)
        acc = jnp.zeros((DH + 16, QB), jnp.float32)
        for c in range(2):
            rows = slice(c * KC, (c + 1) * KC)
            shift = bias_ref[c * 8:(c + 1) * 8, pl.ds(start, QB)] - jnp.maximum(top, NEG / 2)
            x = x_s[rows].reshape(8, HALF, QB) * C1 + shift[:, None, :]
            low = jnp.exp2(x).reshape(KC, QB).astype(jnp.bfloat16)
            e_ref[rows, pl.ds(start, QB)] = low
            acc = acc + dot(vt_s[:, rows], low, NN)
        acc, mass = acc[:DH], acc[DH:DH + 1]
        if second:
            near_top = near_ref[0, pl.ds(qb, 1)]
            new_top = jnp.maximum(near_top, top)
            fades = jnp.exp2(near_top - new_top), jnp.exp2(top - new_top)
            acc = near_out_ref[:, pl.ds(start, QB)] * fades[0] + acc * fades[1]
            mass = near_ref[1, pl.ds(qb, 1)] * fades[0] + mass * fades[1]
            gt = g_s[pl.ds(start, QB)].astype(jnp.float32).T
            stat_ref[2, pl.ds(qb, 1)] = jnp.sum(gt * acc, axis=0, keepdims=True)
            part_ref[0, pl.ds(qb, 1)] = fades[0]
            part_ref[1, pl.ds(qb, 1)] = fades[1]
            top = new_top
        stat_ref[0, pl.ds(qb, 1)] = top
        stat_ref[1, pl.ds(qb, 1)] = mass
        out_ref[:, pl.ds(start, QB)] = acc

    def pair(i, top):
        top_b = score(2 * i + 1, xb_s)
        finish(2 * i, xa_s, top)
        top_a = score(jnp.minimum(2 * i + 2, 7), xa_s)
        finish(2 * i + 1, xb_s, top_b)
        return top_a

    lax.fori_loop(0, 4, pair, score(0, xa_s), unroll=4)


def grad_kernel(*refs):
    place, kv, q5_ref, g5_ref = refs[0], refs[1:5], *refs[5:7]
    e_refs, part_ref, acc_ref = refs[7:9], refs[9], refs[10]
    stats = refs[11:15]
    keep_ref, send_ref, dk_ref, dv_ref = refs[15:19]
    o5_s, dq5_s, kt_s, dk_s, dv_s, delta_s, fade_s = refs[19:26]
    q_s, g_s = q5_ref.reshape(2048, DH), g5_ref.reshape(2048, DH)
    o_s, dq_s = o5_s.reshape(2048, DH), dq5_s.reshape(2048, DH)
    for j in range(4):
        kt_s[:, j * KC:(j + 1) * KC] = kv[j][:, 0].reshape(KC, DH).T
    tops, masses, deltas = [[s[n] for s in stats] for n in range(3)]
    top = jnp.maximum(jnp.maximum(tops[0], tops[1]), jnp.maximum(tops[2], tops[3]))
    fades = [jnp.exp2(t - top) for t in tops]
    mass = sum(m * f for m, f in zip(masses, fades))
    inv_mass = 1.0 / mass
    delta_s[...] = sum(d * f for d, f in zip(deltas, fades)) * inv_mass
    fade_s[...] = fades[0] * inv_mass
    dk_s[...] = jnp.zeros_like(dk_s)
    dv_s[...] = jnp.zeros_like(dv_s)

    def block(qb):
        cols = slice(qb * QB, (qb + 1) * QB)
        q, g = q_s[cols], g_s[cols]
        gt = g.astype(jnp.float32).T
        delta, fade = delta_s[qb:qb + 1], fade_s[qb:qb + 1]
        o_s[cols] = (acc_ref[:, cols] * fade).T.astype(jnp.bfloat16)
        dqt = jnp.zeros((DH, QB), jnp.float32)
        for n, c in enumerate(NEAR + FAR):
            rows = slice(c * KC, (c + 1) * KC)
            half = slice(n % 2 * KC, (n % 2 + 1) * KC)
            if n % 2 == 0:
                local = fade * part_ref[n // 2, qb:qb + 1]
                gf = (gt * local).T.astype(jnp.bfloat16)
            e = e_refs[n // 2][half, cols]
            dp = dot(kv[c][:, 1].reshape(KC, DH), g, NT)
            ds = (e.astype(jnp.float32) * ((dp - delta) * local)).astype(jnp.bfloat16)
            dv_s[rows] += dot(e, gf, NN)
            dk_s[rows] += dot(ds, q, NN)
            dqt = dqt + dot(kt_s[:, rows], ds, NN)
        dq_s[cols] = (dqt * SCALE).T.astype(jnp.bfloat16)

    for qb in range(8):
        block(qb)
    for n, rows5 in enumerate((o5_s, dq5_s)):
        for far in range(2):
            keep_ref[n, far] = rows5[place[0] ^ far, :, place[1]]
            send_ref[n, far] = rows5[place[0] ^ far, :, 1 - place[1]]
    dk_ref[...] = (dk_s[...] * SCALE).astype(jnp.bfloat16)
    dv_ref[...] = dv_s[...].astype(jnp.bfloat16)


VM = pl.BlockSpec(memory_space=pltpu.VMEM)
SM = pl.BlockSpec(memory_space=pltpu.SMEM)
PARAMS = pltpu.CompilerParams(vmem_limit_bytes=16 * 1024 * 1024)
ROWS5 = pltpu.VMEM((2, 16, 2, 32, DH), jnp.bfloat16)


def run_stats(rows, kv, bias, *before):
    out_shape = [
        jax.ShapeDtypeStruct((3, 8, QB), jnp.float32),
        jax.ShapeDtypeStruct((DH, 2048), jnp.float32),
        jax.ShapeDtypeStruct((1024, 2048), jnp.bfloat16),
    ]
    if before:
        out_shape.append(jax.ShapeDtypeStruct((2, 8, QB), jnp.float32))
    else:
        out_shape += [jax.ShapeDtypeStruct((2, 16, 2, 32, DH), jnp.bfloat16)] * 2
    return pl.pallas_call(
        stats_kernel,
        out_shape=out_shape,
        in_specs=[VM] * 7 if before else [SM] + [VM] * 7,
        out_specs=[VM] * len(out_shape),
        scratch_shapes=[
            pltpu.VMEM((1024, DH), jnp.bfloat16),
            pltpu.VMEM((DH + 16, 1024), jnp.bfloat16),
            pltpu.VMEM((1024, QB), jnp.float32),
            pltpu.VMEM((1024, QB), jnp.float32),
        ],
        compiler_params=PARAMS,
        name="stats_far" if before else "stats_near",
    )(*rows, *kv, bias, *before)


def run_grads(place, rows, kv, e, part, acc, stats):
    side = jax.ShapeDtypeStruct((2, 2, 16, 32, DH), jnp.bfloat16)
    keys = jax.ShapeDtypeStruct((2048, DH), jnp.bfloat16)
    return pl.pallas_call(
        grad_kernel,
        out_shape=(side, side, keys, keys),
        in_specs=[SM] + [VM] * 14,
        out_specs=(VM,) * 4,
        scratch_shapes=[ROWS5] * 2
        + [pltpu.VMEM((DH, 2048), jnp.bfloat16)]
        + [pltpu.VMEM((2048, DH), jnp.float32)] * 2
        + [pltpu.VMEM((8, QB), jnp.float32)] * 2,
        compiler_params=PARAMS,
        name="grads",
    )(place, *kv, *rows, *e, part, acc, *stats)


def swap(a, j):
    return lax.ppermute(a, "x", [(i, i ^ j) for i in range(4)])


SWAP = [(0, 1), (1, 0)]
HEADS = ("y0", "z")


def per_device(queries, key_vectors, value_vectors, out_grad, key_tiles, tile_count):
    x_at, y1_at, core_at = [lax.axis_index(a) for a in ("x", "y1", "core")]
    head_at = lax.axis_index("y0") * 8 + lax.axis_index("z")
    place = jnp.stack([y1_at, core_at]).astype(jnp.int32)

    away = jnp.array([AWAY[j] for j in NEAR + FAR], jnp.int32)
    tiles = jnp.arange(16, dtype=jnp.int32)
    k_tiles = ((x_at ^ away)[:, None] * 16 + y1_at * 8 + tiles[None, :8]).reshape(32)
    slots = key_tiles.shape[2]
    lists = lax.dynamic_slice(key_tiles, (head_at, x_at * 16, 0), (1, 16, slots))[0]
    counts = lax.dynamic_slice(tile_count, (head_at, x_at * 16), (1, 16))[0]
    live = jnp.arange(slots, dtype=jnp.int32)[None, :] < counts[:, None]
    lists = jnp.where(live, lists, -1)
    hit = jnp.any(lists[None, :, :] == k_tiles[:, None, None], axis=2)
    bias = jnp.repeat(jnp.where(hit, 0.0, NEG).astype(jnp.float32), TILE, axis=1)

    packed = pack(queries, out_grad, key_vectors, value_vectors)
    got = lax.all_to_all(packed, HEADS, split_axis=0, concat_axis=0, tiled=True)
    got, bias = lax.optimization_barrier((got, bias))
    qg_own, kv_own = got[:, 0:2], got[:, 2:4]
    kv = [kv_own] + [swap(kv_own, j) for j in AWAY[1:]]
    qg_far = lax.ppermute(qg_own, "y1", SWAP)
    qg = [
        qg_own,
        lax.ppermute(qg_own, "core", SWAP),
        qg_far,
        lax.ppermute(qg_far, "core", SWAP),
    ]
    near, near_acc, e_near, *full = run_stats(
        [place, *qg], [kv[j] for j in NEAR], bias[:16]
    )
    stat, acc, e_far, part = run_stats(
        full, [kv[j] for j in FAR], bias[16:], near, near_acc
    )
    stats = [
        stat,
        lax.ppermute(stat, "core", SWAP),
        lax.ppermute(stat, "y1", SWAP),
        lax.ppermute(stat, ("core", "y1"), [(i, 3 - i) for i in range(4)]),
    ]
    keep, leave, dk, dv = run_grads(place, full, kv, (e_near, e_far), part, acc, stats)

    def pair(a, b, j):
        rows = slice(512 * j, 512 * (j + 1))
        return jnp.stack([a[rows], b[rows]])

    came = [swap(pair(dk, dv, j), AWAY[j]) for j in (3, 2, 1)]
    near, far = add_core(keep, lax.ppermute(leave, "core", SWAP))
    send = add_up(dk, dv, came, near, lax.ppermute(far, "y1", SWAP))
    back_home = lax.all_to_all(send, HEADS, split_axis=0, concat_axis=0, tiled=True)
    return unpack(back_home)


def add_core_kernel(keep_ref, came_ref, near_ref, far_ref):
    for n in range(2):
        for far, out in enumerate((near_ref, far_ref)):
            total = keep_ref[n, far].astype(jnp.float32) + came_ref[n, far].astype(jnp.float32)
            out[n] = total.astype(out.dtype)


def add_core(keep, came):
    return pl.pallas_call(
        add_core_kernel,
        out_shape=(
            jax.ShapeDtypeStruct((2, 16, 32, DH), jnp.float32),
            jax.ShapeDtypeStruct((2, 16, 32, DH), jnp.bfloat16),
        ),
        in_specs=[VM] * 2,
        out_specs=(VM,) * 2,
        compiler_params=PARAMS,
        name="add_core",
    )(keep, came)


def add_kernel(dk_ref, dv_ref, *refs):
    came, near_ref, far_ref, send_ref = refs[0:3], refs[3], refs[4], refs[5]
    for n in range(2):
        rows = near_ref[n] + far_ref[n].astype(jnp.float32)
        send_ref[:, n] = rows.astype(jnp.bfloat16)
    for n, own in enumerate((dk_ref, dv_ref)):
        total = own[0:512].astype(jnp.float32)
        for part in came:
            total = total + part[n].astype(jnp.float32)
        send_ref[:, 2 + n] = total.astype(jnp.bfloat16).reshape(16, 32, DH)


def add_up(dk, dv, came, near, far):
    return pl.pallas_call(
        add_kernel,
        out_shape=jax.ShapeDtypeStruct((16, 4, 32, DH), jnp.bfloat16),
        in_specs=[VM] * 7,
        out_specs=VM,
        compiler_params=PARAMS,
        name="add_up",
    )(dk, dv, *came, near, far)


def pack_kernel(*refs):
    arrays, out_ref, held, sems = refs[0:4], refs[4], refs[5], refs[6]
    copies = [pltpu.make_async_copy(arrays[n], held.at[n], sems.at[n]) for n in range(4)]
    for copy in copies:
        copy.start()
    for n, copy in enumerate(copies):
        copy.wait()
        for h in range(16):
            out_ref[h, n] = held[n, :, h * DH:(h + 1) * DH]


def pack(*arrays):
    return pl.pallas_call(
        pack_kernel,
        out_shape=jax.ShapeDtypeStruct((16, 4, 32, DH), jnp.bfloat16),
        in_specs=[pl.BlockSpec(memory_space=pl.ANY)] * 4,
        out_specs=VM,
        scratch_shapes=[
            pltpu.VMEM((4, 32, 16 * DH), jnp.bfloat16),
            pltpu.SemaphoreType.DMA((4,)),
        ],
        compiler_params=pltpu.CompilerParams(vmem_limit_bytes=60 * 1024 * 1024),
        name="pack",
    )(*arrays)


def unpack_kernel(src_ref, *refs):
    outs, held, sems = refs[0:4], refs[4], refs[5]
    copies = [pltpu.make_async_copy(held.at[n], outs[n], sems.at[n]) for n in range(4)]
    for n, copy in enumerate(copies):
        for h in range(16):
            held[n, :, h * DH:(h + 1) * DH] = src_ref[h, n]
        copy.start()
    for copy in copies:
        copy.wait()


def unpack(a):
    rows = jax.ShapeDtypeStruct((32, 16 * DH), jnp.bfloat16)
    return pl.pallas_call(
        unpack_kernel,
        out_shape=(rows,) * 4,
        in_specs=[VM],
        out_specs=(pl.BlockSpec(memory_space=pl.ANY),) * 4,
        scratch_shapes=[
            pltpu.VMEM((4, 32, 16 * DH), jnp.bfloat16),
            pltpu.SemaphoreType.DMA((4,)),
        ],
        compiler_params=PARAMS,
        name="unpack",
    )(a)


def solution(mesh):
    grid = jax.sharding.Mesh(mesh.devices.reshape(8, 2, 4, 2, 2), ("z", "core", "x", "y1", "y0"))
    rows = P(("x", "y1", "y0", "z", "core"), None)
    return jax.shard_map(
        per_device,
        mesh=grid,
        in_specs=(rows, rows, rows, rows, P(), P()),
        out_specs=(rows,) * 4,
        check_vma=False,
    )
```
